512 devices in a mesh: lon: 32 (over y, z_lo, core), lat: 16 (over x, z_hi).
Axes of the slice: x: 4, y: 4, z: 16 (z_hi: 4, z_lo: 4; z = z_hi * 4 + z_lo), core: 2. Of those that a mesh axis runs over, the one named last changes fastest.
Arguments:
- velocity: float32 [2, 768, 4096], P(None, 'lat', 'lon'), may hold values from -6 to 6
- stress: float32 [3, 768, 4096], P(None, 'lat', 'lon'), may hold values from -6 to 6
- strength: float32 [768, 4096], P('lat', 'lon'), may hold values from 0.3 to 3
- wind_stress: bfloat16 [2, 768, 4096], P(None, 'lat', 'lon'), may hold values from -6 to 6
- ice_mask: int32 [768, 4096], P('lat', 'lon'), may hold values from 0 to 1, as said below
- start_step: int32 [1], replicated, may hold values from 0 to 114
- velocity_cotangent: float32 [2, 768, 4096], P(None, 'lat', 'lon'), may hold values from -6 to 6
Outputs:
- final_velocity: float32 [2, 768, 4096], P(None, 'lat', 'lon')
- velocity_gradient: float32 [2, 768, 4096], P(None, 'lat', 'lon')
- stress_gradient: float32 [3, 768, 4096], P(None, 'lat', 'lon')
The draws below stay inside these ranges and needn't reach their ends.
Inputs may be any that keep to these rules, and one draw needn't show every extreme that they name: `ice_mask`: 0 or 1 in every cell.
All inputs are finite; a program needn't handle non-finite values.
Results may differ from the reference program's by a relative error of at most 0.00045.
Values sent between devices are 32-bit elements; how exact they have to be, the bound alone decides.
A program may use at most 64 MiB of HBM per device.

```python
import math
from functools import partial
import jax
import jax.numpy as jnp

NSUB = 6
EVP_TOTAL = 120
NX = 4096
NY = 768


def draw_ice_mask(key, part):
    key = jax.random.fold_in(key, 7)
    row_index = jnp.arange(NY, dtype=jnp.int32)
    percent = 30 + 60 * jnp.abs(2 * row_index + 1 - NY) // NY
    chance = jax.random.randint(key, (NY, NX), 0, 100, dtype=jnp.int32)
    return (chance < percent[:, None]).astype(jnp.int32)


def steps_of(rng, dims, shards, least, high):
    level, own = 1.0, jax.random.fold_in(rng, 6)
    for axis_at, blocks in shards:
        draws = jnp.exp(jax.random.uniform(jax.random.fold_in(own, axis_at), (blocks,), jnp.float32, least / len(shards), high / len(shards)))
        level = level * jnp.repeat(draws, dims[axis_at] // blocks).reshape([-1 if axis == axis_at else 1 for axis in range(len(dims))])
    return level


def bell_draw(key, dims, scale, reach, shards=(), kind=jnp.bfloat16):
    drawn = jax.random.normal(key, dims, jnp.float32) * scale
    if len(shards) > 0:
        drawn = steps_of(key, dims, shards, -0.22, 0.18) * drawn
    return jnp.clip(drawn, min=-reach, max=reach).astype(kind)


def setup_inputs(seed: int = 0) -> dict:
    key_list = jax.random.split(jax.random.key(seed), 8)
    velocity = bell_draw(key_list[0], (2, NY, NX), 1.0, 6.0, ((1, 16), (2, 32)), jnp.float32)
    stress = bell_draw(key_list[1], (3, NY, NX), 1.0, 6.0, ((1, 16), (2, 32)), jnp.float32)
    strength = jnp.clip(jnp.exp(math.log(3.0) - 2.3025851 * jax.random.uniform(key_list[2], (NY, NX), jnp.float32) ** steps_of(key_list[2], (NY, NX), ((0, 16), (1, 32)), -0.2, 0.2)), 0.3, 3.0)
    wind_stress = bell_draw(key_list[3], (2, NY, NX), 1.0, 6.0, ((1, 16), (2, 32)))
    ice_mask = draw_ice_mask(jax.random.fold_in(key_list[7], 71), 0)
    start_step = jax.random.randint(key_list[5], (1,), 0, EVP_TOTAL - NSUB + 1).astype(jnp.int32)
    velocity_cotangent = bell_draw(key_list[6], (2, NY, NX), 1.0, 6.0, ((1, 16), (2, 32)), jnp.float32)
    return {"velocity": velocity, "stress": stress, "strength": strength, "wind_stress": wind_stress, "ice_mask": ice_mask, "start_step": start_step, "velocity_cotangent": velocity_cotangent}


relax_rate = 0.5
step_factor = 0.5
drag_rate = 1.0
ellipse_sq = 4.0
delta_min_sq = 0.25

def stress_update(stress_old, vel_west, vel_east, vel_south, vel_north, strength, ice_cover):
    strain_xx = 0.5 * (vel_east[0] - vel_west[0])
    strain_yy = 0.5 * (vel_north[1] - vel_south[1])
    shear_rate = 0.5 * (vel_north[0] - vel_south[0]) + 0.5 * (vel_east[1] - vel_west[1])
    divergence = strain_xx + strain_yy
    tension = strain_xx - strain_yy
    delta_norm = jnp.sqrt(divergence * divergence + (tension * tension + shear_rate * shear_rate) / ellipse_sq + delta_min_sq)
    viscous_ratio = strength / delta_norm
    target = jnp.stack([viscous_ratio * divergence - strength, viscous_ratio * tension / ellipse_sq, 0.5 * viscous_ratio * shear_rate / ellipse_sq])
    return (stress_old + relax_rate * target) / (1.0 + relax_rate) * ice_cover

def velocity_update(velocity, xx_west, xx_east, xy_west, xy_east, yy_south, yy_north, xy_south, xy_north, wind_force, weight, coriolis, ice_cover):
    force_x = 0.5 * (xx_east - xx_west) + 0.5 * (xy_north - xy_south)
    force_y = 0.5 * (xy_east - xy_west) + 0.5 * (yy_north - yy_south)
    right_u = velocity[0] + step_factor * (force_x + weight * wind_force[0])
    right_v = velocity[1] + step_factor * (force_y + weight * wind_force[1])
    diag_term = 1.0 + step_factor * drag_rate
    turn_term = step_factor * coriolis
    det_term = diag_term * diag_term + turn_term * turn_term
    return jnp.stack([(diag_term * right_u + turn_term * right_v) / det_term, (diag_term * right_v - turn_term * right_u) / det_term]) * ice_cover

def northward(values, fold_sign):
    fold_row = fold_sign * jnp.flip(values[:, -1:, :], axis=2)
    return jnp.concatenate([values[:, 1:, :], fold_row], axis=1)

def southward(values):
    return jnp.concatenate([jnp.zeros_like(values[:, :1, :]), values[:, :-1, :]], axis=1)

def subcycle(velocity, stress_old, strength, ice_cover, wind_force, weight, coriolis):
    stress_new = stress_update(stress_old, jnp.roll(velocity, 1, axis=2), jnp.roll(velocity, -1, axis=2), southward(velocity), northward(velocity, -1.0), strength, ice_cover)
    normal_xx = 0.5 * (stress_new[0] + stress_new[1])
    normal_yy = 0.5 * (stress_new[0] - stress_new[1])
    lon_pair = jnp.stack([normal_xx, stress_new[2]])
    lat_pair = jnp.stack([normal_yy, stress_new[2]])
    from_west = jnp.roll(lon_pair, 1, axis=2)
    from_east = jnp.roll(lon_pair, -1, axis=2)
    from_south = southward(lat_pair)
    from_north = northward(lat_pair, 1.0)
    velocity_new = velocity_update(velocity, from_west[0], from_east[0], from_west[1], from_east[1], from_south[0], from_north[0], from_south[1], from_north[1], wind_force, weight, coriolis, ice_cover)
    return (velocity_new, stress_new)

def reference(velocity, stress, strength, wind_stress, ice_mask, start_step, velocity_cotangent):
    ice_cover = ice_mask.astype(jnp.float32)
    wind_force = wind_stress.astype(jnp.float32)
    row_values = jnp.arange(NY).astype(jnp.float32)
    coriolis = (1.2 * ((2.0 * row_values + 1.0) / NY - 1.0))[:, None]
    start_value = start_step[0].astype(jnp.float32)
    saved_steps = []
    vel_now, stress_now = (velocity, stress)
    for step_index in range(NSUB):
        weight = (start_value + (step_index + 1)) / EVP_TOTAL
        saved_steps.append((vel_now, stress_now, weight))
        vel_now, stress_now = subcycle(vel_now, stress_now, strength, ice_cover, wind_force, weight, coriolis)
    vel_grad = velocity_cotangent
    stress_grad = jnp.zeros_like(stress)
    for step_index in reversed(range(NSUB)):
        vel_old, stress_old, weight = saved_steps[step_index]
        stepper = partial(subcycle, strength=strength, ice_cover=ice_cover, wind_force=wind_force, weight=weight, coriolis=coriolis)
        _, pull_back = jax.vjp(stepper, vel_old, stress_old)
        vel_grad, stress_grad = pull_back((vel_grad, stress_grad))
    return (vel_now, vel_grad, stress_grad)
```

```python
from functools import partial

import jax
import jax.numpy as jnp
from jax import lax
from jax.experimental import pallas as pl
from jax.experimental.pallas import tpu as pltpu
from jax.sharding import PartitionSpec as P

NSUB = 6
EVP_TOTAL = 120
MESH = pl.DeviceIdType.MESH

ROWS = 48
COLS = 128
PAD = 24
EXT = ROWS + 2 * PAD
REACH = 22
BACK = 12
NFLD = 11
NMAIN = 9
SLOT = 24

ODD_FIELDS = (0, 1, 7, 8, 9, 10)


def slot_of(field):
    if field < 5:
        return 0, SLOT * field, SLOT
    if field < NMAIN:
        return 1, SLOT * (field - 5), SLOT
    return 1, 4 * SLOT + BACK * (field - NMAIN), BACK


def lane_ids(shape):
    return lax.broadcasted_iota(jnp.int32, shape, len(shape) - 1)


def gather_kernel(
    lon_count,
    lat_count,
    vel,
    sig,
    strength,
    wind,
    mask,
    cot,
    ext,
    land,
    sig_in,
    str_in,
    wind_in,
    mask_in,
    pack,
    local_sem,
    send_sem,
    recv_sem,
    self_sem,
):
    lon = lax.axis_index("lon")
    lat = lax.axis_index("lat")
    top = lat == lat_count - 1
    bottom = lat == 0
    west = lax.rem(lon + lon_count - 1, lon_count)
    east = lax.rem(lon + 1, lon_count)
    up = jnp.where(top, lat, lat + 1)
    down = jnp.where(bottom, lat, lat - 1)
    north_lon = jnp.where(top, lon_count - 1 - lon, lon)
    north_a = jnp.where(top, lax.rem(lon_count - lon, lon_count), west)
    north_b = jnp.where(top, lax.rem(2 * lon_count - 2 - lon, lon_count), east)
    self_a = jnp.logical_and(top, north_a == lon)
    self_b = jnp.logical_and(top, north_b == lon)

    barrier = pltpu.get_barrier_semaphore()

    def greet(dev_lon, dev_lat):
        pl.semaphore_signal(barrier, inc=1, device_id=(dev_lon, dev_lat), device_id_type=MESH)

    greet(west, lat)
    greet(east, lat)
    greet(north_lon, up)
    pl.when(jnp.logical_not(self_a))(lambda: greet(north_a, up))
    pl.when(jnp.logical_not(self_b))(lambda: greet(north_b, up))

    @pl.when(jnp.logical_not(bottom))
    def _():
        greet(lon, down)
        greet(west, down)
        greet(east, down)

    own = pl.ds(PAD, ROWS)
    loads = [
        pltpu.make_async_copy(vel, ext.at[pl.ds(0, 2), own], local_sem.at[0]),
        pltpu.make_async_copy(sig, sig_in, local_sem.at[1]),
        pltpu.make_async_copy(strength, str_in, local_sem.at[2]),
        pltpu.make_async_copy(wind, wind_in, local_sem.at[3]),
        pltpu.make_async_copy(mask, mask_in, local_sem.at[4]),
        pltpu.make_async_copy(cot, ext.at[pl.ds(NMAIN, 2), own], local_sem.at[5]),
    ]
    for copy in loads:
        copy.start()
    for copy in loads:
        copy.wait()

    cover = mask_in[...].astype(jnp.float32)
    ext[2, own] = 0.125 * (sig_in[0] + sig_in[1])
    ext[3, own] = 0.125 * (sig_in[0] - sig_in[1])
    ext[4, own] = 0.25 * sig_in[2]
    ext[5, own] = (1.0 / 24.0) * cover * str_in[...]
    ext[6, own] = cover * (1.0 / 1.5)
    ext[7, own] = wind_in[0].astype(jnp.float32)
    ext[8, own] = wind_in[1].astype(jnp.float32)

    lanes = lane_ids((ROWS, COLS))
    for side in range(2):
        for plane in range(2):
            packed = None
            for field in range(NFLD):
                at_plane, first, width = slot_of(field)
                if at_plane != plane:
                    continue
                begin = 0 if side == 0 else COLS - width
                value = ext[field, own]
                shift = (first - begin) % COLS
                if shift:
                    value = pltpu.roll(value, shift, 1)
                packed = value if packed is None else jnp.where(lanes < first, packed, value)
            pack[side, plane] = packed

    @pl.when(bottom)
    def _():
        ext[:, pl.ds(0, PAD)] = jnp.zeros((NFLD, PAD, COLS), jnp.float32)
        land[:, :, pl.ds(0, PAD)] = jnp.zeros((2, 2, PAD, COLS), jnp.float32)

    count = (
        3
        + jnp.where(self_a, 0, 1)
        + jnp.where(self_b, 0, 1)
        + jnp.where(bottom, 0, 3)
    )
    pl.semaphore_wait(barrier, count)

    def send(src, dst, slot, sem, dev_lon, dev_lat):
        return pltpu.make_async_remote_copy(
            src_ref=src,
            dst_ref=dst,
            send_sem=send_sem.at[slot],
            recv_sem=recv_sem.at[sem],
            device_id=(dev_lon, dev_lat),
            device_id_type=MESH,
        )

    main = pl.ds(0, NMAIN)
    tail = pl.ds(NMAIN, 2)
    def north_sends(row_main, row_tail, sem):
        return (
            send(ext.at[main, pl.ds(PAD + ROWS - REACH, REACH)], ext.at[main, pl.ds(row_main, REACH)], 0, sem, north_lon, up),
            send(ext.at[tail, pl.ds(PAD + ROWS - BACK, BACK)], ext.at[tail, pl.ds(row_tail, BACK)], 1, sem + 1, north_lon, up),
        )

    def north_strip(side, row, sem, dev_lon):
        return send(
            pack.at[side, :, pl.ds(ROWS - REACH, REACH)], land.at[side, :, pl.ds(row, REACH)], 2 + side, sem, dev_lon, up
        )

    def north_self(side):
        return pltpu.make_async_copy(
            pack.at[side, :, pl.ds(ROWS - REACH, REACH)],
            land.at[side, :, pl.ds(EXT - REACH, REACH)],
            self_sem.at[side],
        )

    south_sends = (
        send(ext.at[main, pl.ds(PAD, REACH)], ext.at[main, pl.ds(PAD + ROWS, REACH)], 4, 2, lon, down),
        send(ext.at[tail, pl.ds(PAD, BACK)], ext.at[tail, pl.ds(PAD + ROWS, BACK)], 5, 3, lon, down),
        send(pack.at[0, :, pl.ds(0, REACH)], land.at[0, :, pl.ds(PAD + ROWS, REACH)], 6, 4, west, down),
        send(pack.at[1, :, pl.ds(0, REACH)], land.at[1, :, pl.ds(PAD + ROWS, REACH)], 7, 5, east, down),
    )
    lon_sends = (
        send(pack.at[0], land.at[0, :, own], 8, 0, west, lat),
        send(pack.at[1], land.at[1, :, own], 9, 1, east, lat),
    )
    low = north_sends(PAD - REACH, PAD - BACK, 6)
    fold = north_sends(EXT - REACH, EXT - BACK, 2)
    low_strips = (north_strip(0, PAD - REACH, 8, north_a), north_strip(1, PAD - REACH, 9, north_b))
    fold_strips = (north_strip(0, EXT - REACH, 4, north_a), north_strip(1, EXT - REACH, 5, north_b))

    @pl.when(jnp.logical_not(top))
    def _():
        for copy in low + low_strips:
            copy.start()

    @pl.when(top)
    def _():
        for copy in fold:
            copy.start()
        for side, is_self in ((0, self_a), (1, self_b)):
            pl.when(is_self)(lambda side=side: north_self(side).start())
            pl.when(jnp.logical_not(is_self))(lambda side=side: fold_strips[side].start())

    @pl.when(jnp.logical_not(bottom))
    def _():
        for copy in south_sends:
            copy.start()

    for copy in lon_sends:
        copy.start()

    lon_sends[0].wait_recv()
    lon_sends[1].wait_recv()
    south_sends[0].wait_recv()
    south_sends[1].wait_recv()
    for side, is_self in ((0, self_a), (1, self_b)):
        pl.when(is_self)(lambda side=side: north_self(side).wait())
        pl.when(jnp.logical_not(is_self))(lambda side=side: south_sends[2 + side].wait_recv())

    @pl.when(jnp.logical_not(bottom))
    def _():
        for copy in low + low_strips:
            copy.wait_recv()
        for copy in south_sends:
            copy.wait_send()

    for copy in low:
        copy.wait_send()
    for side, is_self in ((0, self_a), (1, self_b)):
        pl.when(jnp.logical_not(is_self))(lambda side=side: low_strips[side].wait_send())
    for copy in lon_sends:
        copy.wait_send()


def gather_halos(lon_count, lat_count, *operands):
    f32 = jnp.float32
    return pl.pallas_call(
        partial(gather_kernel, lon_count, lat_count),
        out_shape=(
            jax.ShapeDtypeStruct((NFLD, EXT, COLS), f32),
            jax.ShapeDtypeStruct((2, 2, EXT, COLS), f32),
        ),
        in_specs=[pl.BlockSpec(memory_space=pl.ANY)] * 6,
        out_specs=(
            pl.BlockSpec(memory_space=pltpu.VMEM),
            pl.BlockSpec(memory_space=pltpu.VMEM),
        ),
        scratch_shapes=[
            pltpu.VMEM((3, ROWS, COLS), f32),
            pltpu.VMEM((ROWS, COLS), f32),
            pltpu.VMEM((2, ROWS, COLS), jnp.bfloat16),
            pltpu.VMEM((ROWS, COLS), jnp.int32),
            pltpu.VMEM((2, 2, ROWS, COLS), f32),
            pltpu.SemaphoreType.DMA((6,)),
            pltpu.SemaphoreType.DMA((10,)),
            pltpu.SemaphoreType.DMA((10,)),
            pltpu.SemaphoreType.DMA((2,)),
        ],
        compiler_params=pltpu.CompilerParams(
            collective_id=0, has_side_effects=True, vmem_limit_bytes=32 * 1024 * 1024
        ),
    )(*operands)


TILE = 8


def tiles_for(reach):
    low = (PAD - reach) // TILE
    high = -(-(PAD + ROWS + reach) // TILE)
    return range(low * TILE, high * TILE, TILE)


def flip_tile(value):
    lane = lane_ids(value.shape)
    bit = 1
    while bit < COLS:
        value = jnp.where((lane & bit) != 0, pltpu.roll(value, bit, 1), pltpu.roll(value, COLS - bit, 1))
        bit *= 2
    row = lax.broadcasted_iota(jnp.int32, value.shape, 0)
    bit = 1
    while bit < TILE:
        value = jnp.where((row & bit) != 0, pltpu.roll(value, bit, 0), pltpu.roll(value, TILE - bit, 0))
        bit *= 2
    return value


def evp_kernel(
    lat_count,
    start,
    ext,
    land,
    final_vel,
    vel_grad,
    sig_grad,
    fld,
    state,
    turn,
    saved,
    back,
    strain,
    carry,
):
    top = lax.axis_index("lat") == lat_count - 1
    band = lax.axis_index("lat")
    shape = (TILE, COLS)
    lane = lane_ids(shape)
    first_lane = lane == 0
    last_lane = lane == COLS - 1
    west_half = lane < COLS // 2

    for r in range(0, EXT, TILE):
        rows = pl.ds(r, TILE)
        for field in range(NFLD):
            plane, first, width = slot_of(field)
            a = land[0, plane, rows]
            b = land[1, plane, rows]
            shift_a = (-first) % COLS
            shift_b = (COLS - width - first) % COLS
            if shift_a:
                a = pltpu.roll(a, shift_a, 1)
            if shift_b:
                b = pltpu.roll(b, shift_b, 1)
            fld[field, 0, rows] = ext[field, rows]
            fld[field, 1, rows] = jnp.where(west_half, a, b)

    @pl.when(top)
    def _():
        def one(i, _):
            odd = (i < 2) | (i >= 7)
            sign = jnp.where(odd, -1.0, 1.0)
            for plane in range(2):
                old = [fld[i, plane, pl.ds(PAD + ROWS + t * TILE, TILE)] for t in range(3)]
                for t in range(3):
                    fld[i, plane, pl.ds(PAD + ROWS + t * TILE, TILE)] = sign * flip_tile(old[2 - t])
            return 0

        lax.fori_loop(0, NFLD, one, 0)

    for r in range(0, EXT, TILE):
        rows = pl.ds(r, TILE)
        row = band * ROWS + (r - PAD) + lax.broadcasted_iota(jnp.int32, shape, 0)
        total = ROWS * lat_count
        row = jnp.where(row >= total, 2 * total - 1 - row, row).astype(jnp.float32)
        half_f = 0.6 * ((2.0 * row + 1.0) / total - 1.0)
        scale = 1.5 / (2.25 + half_f * half_f)
        for plane in range(2):
            cover = fld[6, plane, rows]
            turn[0, plane, rows] = cover * (1.5 * scale)
            turn[1, plane, rows] = cover * (half_f * scale)

    def at(ref, lead, plane, r):
        if r < 0:
            return pltpu.roll(ref[lead + (plane, pl.ds(0, TILE))], 1, 0)
        if r > EXT - TILE:
            return pltpu.roll(ref[lead + (plane, pl.ds(EXT - TILE, TILE))], TILE - 1, 0)
        return ref[lead + (plane, pl.ds(r, TILE))]

    def lat_diff(ref, lead, r):
        return [at(ref, lead, p, r + 1) - at(ref, lead, p, r - 1) for p in range(2)]

    def lon_diff(ref, lead, r):
        here = [at(ref, lead, p, r) for p in range(2)]
        east = [pltpu.roll(x, COLS - 1, 1) for x in here]
        west = [pltpu.roll(x, 1, 1) for x in here]
        return [
            jnp.where(last_lane, east[1 - p], east[p]) - jnp.where(first_lane, west[1 - p], west[p])
            for p in range(2)
        ]

    start_value = start[0].astype(jnp.float32)
    for k in range(NSUB):
        src = fld if k == 0 else state
        left = NSUB - 1 - k
        keep = set(tiles_for(2 * k + 1))
        for r in tiles_for(11 + 2 * left):
            rows = pl.ds(r, TILE)
            dux = lon_diff(src, (0,), r)
            dvx = lon_diff(src, (1,), r)
            duy = lat_diff(src, (0,), r)
            dvy = lat_diff(src, (1,), r)
            for p in range(2):
                div = dux[p] + dvy[p]
                ten = dux[p] - dvy[p]
                she = duy[p] + dvx[p]
                inv = lax.rsqrt(div * div + 0.25 * (ten * ten + she * she) + 1.0)
                part = fld[5, p, rows]
                div = div * inv
                inv4 = 0.25 * inv
                ten = ten * inv4
                she = she * inv4
                if r in keep:
                    saved[k, 0, p, rows] = div
                    saved[k, 1, p, rows] = ten
                    saved[k, 2, p, rows] = she
                    saved[k, 3, p, rows] = part * inv
                cover = fld[6, p, rows]
                pull = div - 1.0
                state[2, p, rows] = cover * src[2, p, rows] + part * (pull + ten)
                state[3, p, rows] = cover * src[3, p, rows] + part * (pull - ten)
                state[4, p, rows] = cover * src[4, p, rows] + part * she
        weight = 0.5 * ((start_value + (k + 1)) / EVP_TOTAL)
        for r in tiles_for(0 if left == 0 else 10 + 2 * left):
            rows = pl.ds(r, TILE)
            dxx = lon_diff(state, (2,), r)
            dxy = lon_diff(state, (4,), r)
            dyx = lat_diff(state, (4,), r)
            dyy = lat_diff(state, (3,), r)
            for p in range(2):
                ru = src[0, p, rows] + (dxx[p] + dyx[p]) + weight * fld[7, p, rows]
                rv = src[1, p, rows] + (dxy[p] + dyy[p]) + weight * fld[8, p, rows]
                ca = turn[0, p, rows]
                cb = turn[1, p, rows]
                un = ca * ru + cb * rv
                vn = ca * rv - cb * ru
                if left == 0:
                    if p == 0:
                        final_vel[0, pl.ds(r - PAD, TILE)] = un
                        final_vel[1, pl.ds(r - PAD, TILE)] = vn
                else:
                    state[0, p, rows] = un
                    state[1, p, rows] = vn

    for r in tiles_for(BACK):
        rows = pl.ds(r, TILE)
        for p in range(2):
            gu = fld[9, p, rows]
            gv = fld[10, p, rows]
            ca = turn[0, p, rows]
            cb = turn[1, p, rows]
            back[0, p, rows] = ca * gu - cb * gv
            back[1, p, rows] = cb * gu + ca * gv

    for k in reversed(range(NSUB)):
        for r in tiles_for(2 * k + 1):
            rows = pl.ds(r, TILE)
            dux = lon_diff(back, (0,), r)
            dvx = lon_diff(back, (1,), r)
            duy = lat_diff(back, (0,), r)
            dvy = lat_diff(back, (1,), r)
            for p in range(2):
                gx = -dux[p]
                gy = -dvy[p]
                gz = -(duy[p] + dvx[p])
                if k < NSUB - 1:
                    gx = carry[0, p, rows] + gx
                    gy = carry[1, p, rows] + gy
                    gz = carry[2, p, rows] + gz
                both = gx + gy
                apart = gx - gy
                cover = fld[6, p, rows]
                if k > 0:
                    carry[0, p, rows] = cover * gx
                    carry[1, p, rows] = cover * gy
                    carry[2, p, rows] = cover * gz
                elif p == 0 and PAD <= r < PAD + ROWS:
                    out = pl.ds(r - PAD, TILE)
                    c8 = 0.125 * cover
                    sig_grad[0, out] = c8 * both
                    sig_grad[1, out] = c8 * apart
                    sig_grad[2, out] = (0.25 * cover) * gz
                div = saved[k, 0, p, rows]
                ten = saved[k, 1, p, rows]
                she = saved[k, 2, p, rows]
                part = saved[k, 3, p, rows]
                along = both * div + apart * ten + gz * she
                g_div = part * (both - along * div)
                g_ten = part * (0.25 * apart - along * ten)
                strain[0, p, rows] = g_div + g_ten
                strain[1, p, rows] = g_div - g_ten
                strain[2, p, rows] = part * (0.25 * gz - along * she)
        for r in tiles_for(2 * k):
            rows = pl.ds(r, TILE)
            dax = lon_diff(strain, (0,), r)
            dsx = lon_diff(strain, (2,), r)
            dsy = lat_diff(strain, (2,), r)
            dby = lat_diff(strain, (1,), r)
            for p in range(2):
                gu = back[0, p, rows] - (dax[p] + dsy[p])
                gv = back[1, p, rows] - (dsx[p] + dby[p])
                if k > 0:
                    ca = turn[0, p, rows]
                    cb = turn[1, p, rows]
                    back[0, p, rows] = ca * gu - cb * gv
                    back[1, p, rows] = cb * gu + ca * gv
                elif p == 0:
                    vel_grad[0, pl.ds(r - PAD, TILE)] = gu
                    vel_grad[1, pl.ds(r - PAD, TILE)] = gv


def evp_and_adjoint(lat_count, start, ext, land):
    f32 = jnp.float32
    vmem = pl.BlockSpec(memory_space=pltpu.VMEM)
    return pl.pallas_call(
        partial(evp_kernel, lat_count),
        out_shape=(
            jax.ShapeDtypeStruct((2, ROWS, COLS), f32),
            jax.ShapeDtypeStruct((2, ROWS, COLS), f32),
            jax.ShapeDtypeStruct((3, ROWS, COLS), f32),
        ),
        in_specs=[pl.BlockSpec(memory_space=pltpu.SMEM), vmem, vmem],
        out_specs=(vmem, vmem, vmem),
        scratch_shapes=[
            pltpu.VMEM((NFLD, 2, EXT, COLS), f32),
            pltpu.VMEM((5, 2, EXT, COLS), f32),
            pltpu.VMEM((2, 2, EXT, COLS), f32),
            pltpu.VMEM((NSUB, 4, 2, EXT, COLS), f32),
            pltpu.VMEM((2, 2, EXT, COLS), f32),
            pltpu.VMEM((3, 2, EXT, COLS), f32),
            pltpu.VMEM((3, 2, EXT, COLS), f32),
        ],
        compiler_params=pltpu.CompilerParams(vmem_limit_bytes=32 * 1024 * 1024),
    )(start, ext, land)


def shards(lon_count, lat_count, velocity, stress, strength, wind_stress, ice_mask, start_step, velocity_cotangent):
    ext, land = gather_halos(
        lon_count, lat_count, velocity, stress, strength, wind_stress, ice_mask, velocity_cotangent
    )
    return evp_and_adjoint(lat_count, start_step, ext, land)


def solution(mesh):
    placed = (
        P(None, "lat", "lon"),
        P(None, "lat", "lon"),
        P("lat", "lon"),
        P(None, "lat", "lon"),
        P("lat", "lon"),
        P(),
        P(None, "lat", "lon"),
    )
    return jax.shard_map(
        partial(shards, mesh.shape["lon"], mesh.shape["lat"]),
        mesh=mesh,
        in_specs=placed,
        out_specs=(P(None, "lat", "lon"), P(None, "lat", "lon"), P(None, "lat", "lon")),
        check_vma=False,
    )
```

```python
from functools import partial

import jax
import jax.numpy as jnp
from jax import lax
from jax.experimental import pallas as pl
from jax.experimental.pallas import tpu as pltpu
from jax.sharding import PartitionSpec as P

NSUB = 6
EVP_TOTAL = 120
MESH = pl.DeviceIdType.MESH
VMEM_LIMIT = 60 * 1024 * 1024

ROWS = 48
COLS = 128
PAD = 24
EXT = ROWS + 2 * PAD
REACH = 22
BACK = 12
NFLD = 11
NMAIN = 9
SLOT = 24

ODD_FIELDS = (0, 1, 7, 8, 9, 10)


def slot_of(field):
    if field < 5:
        return 0, SLOT * field, SLOT
    if field < NMAIN:
        return 1, SLOT * (field - 5), SLOT
    return 1, 4 * SLOT + BACK * (field - NMAIN), BACK


def lane_ids(shape):
    return lax.broadcasted_iota(jnp.int32, shape, len(shape) - 1)


def start_order(lon, lat):
    y = lax.div(lon, 8)
    z_low = lax.rem(lax.div(lon, 2), 4)
    x = lax.div(lat, 4)
    z_high = lax.rem(lat, 4)
    early_half = z_high < 2
    base = jnp.where(early_half, 44 * z_high, 96 - 4 * z_high)
    step = jnp.where(early_half, 13, 4)
    return 1024 * (7 * x + 7 * y + base + step * z_low) + 32 * lat + lon


def gather_kernel(
    lon_count,
    lat_count,
    vel,
    sig,
    strength,
    wind,
    mask,
    cot,
    ext,
    land,
    wind_in,
    mask_in,
    vel_in,
    sig_in,
    str_in,
    cot_in,
    made,
    pack,
    local_sem,
    send_sem,
    recv_sem,
    self_sem,
    ready,
):
    lon = lax.axis_index("lon")
    lat = lax.axis_index("lat")
    top = lat == lat_count - 1
    inner = jnp.logical_not(top)
    has_south = lat > 0
    west = lax.rem(lon + lon_count - 1, lon_count)
    east = lax.rem(lon + 1, lon_count)
    up = jnp.where(top, lat, lat + 1)
    down = jnp.where(has_south, lat - 1, lat)
    north_lon = jnp.where(top, lon_count - 1 - lon, lon)
    north_a = jnp.where(top, lax.rem(lon_count - lon, lon_count), west)
    north_b = jnp.where(top, lax.rem(2 * lon_count - 2 - lon, lon_count), east)
    self_a = jnp.logical_and(top, north_a == lon)
    self_b = jnp.logical_and(top, north_b == lon)
    always = lat >= 0

    W, E, N, NA, NB, S, SA, SB = range(8)
    partner = [
        (west, lat),
        (east, lat),
        (north_lon, up),
        (north_a, up),
        (north_b, up),
        (lon, down),
        (west, down),
        (east, down),
    ]
    there = [always, always, always, jnp.logical_not(self_a), jnp.logical_not(self_b), has_south, has_south, has_south]
    reverse = [
        E,
        W,
        jnp.where(top, N, S),
        jnp.where(top, NA, SB),
        jnp.where(top, NB, SA),
        N,
        NB,
        NA,
    ]
    mine = start_order(lon, lat)
    later = [start_order(*p) > mine for p in partner]
    greets = [jnp.logical_and(t, l) for t, l in zip(there, later)]
    greeted = [jnp.logical_and(t, jnp.logical_not(l)) for t, l in zip(there, later)]

    barrier = pltpu.get_barrier_semaphore()
    for link in range(8):

        @pl.when(greets[link])
        def _(link=link):
            pl.semaphore_signal(barrier, inc=1, device_id=partner[link], device_id_type=MESH)

    own = pl.ds(PAD, ROWS)
    loads = [
        pltpu.make_async_copy(wind, wind_in, local_sem.at[0]),
        pltpu.make_async_copy(mask, mask_in, local_sem.at[1]),
        pltpu.make_async_copy(vel, vel_in, local_sem.at[2]),
        pltpu.make_async_copy(sig, sig_in, local_sem.at[3]),
        pltpu.make_async_copy(strength, str_in, local_sem.at[4]),
        pltpu.make_async_copy(cot, cot_in, local_sem.at[5]),
    ]
    for copy in loads:
        copy.start()

    def send(src, dst, slot, sem, link):
        return pltpu.make_async_remote_copy(
            src_ref=src,
            dst_ref=dst,
            send_sem=send_sem.at[slot],
            recv_sem=recv_sem.at[sem],
            device_id=partner[link],
            device_id_type=MESH,
        )

    def rows_raw(row_of, to_of, slot, sem, link):
        return [
            send(vel.at[:, pl.ds(row_of(REACH), REACH)], ext.at[pl.ds(0, 2), pl.ds(to_of(REACH), REACH)], slot, sem, link),
            send(
                sig.at[:, pl.ds(row_of(REACH - 1), REACH - 1)],
                ext.at[pl.ds(2, 3), pl.ds(to_of(REACH - 1), REACH - 1)],
                slot + 1,
                sem + 1,
                link,
            ),
            send(
                strength.at[pl.ds(row_of(REACH - 1), REACH - 1)],
                ext.at[5, pl.ds(to_of(REACH - 1), REACH - 1)],
                slot + 2,
                sem + 2,
                link,
            ),
            send(cot.at[:, pl.ds(row_of(BACK), BACK)], ext.at[pl.ds(NMAIN, 2), pl.ds(to_of(BACK), BACK)], slot + 3, sem + 3, link),
        ]

    def rows_made(row_of, to_of, slot, sem, link):
        return send(
            made.at[:, pl.ds(row_of(REACH - 1), REACH - 1)],
            ext.at[pl.ds(6, 3), pl.ds(to_of(REACH - 1), REACH - 1)],
            slot + 4,
            sem + 4,
            link,
        )

    last = lambda n: ROWS - n
    to_low = lambda n: PAD - n
    to_fold = lambda n: EXT - n
    first = lambda n: 0
    to_high = lambda n: PAD + ROWS

    def strip(side, row, to, slot, sem, link):
        return send(pack.at[side, :, pl.ds(row, REACH)], land.at[side, :, pl.ds(to, REACH)], slot, sem, link)

    def self_strip(side):
        return pltpu.make_async_copy(
            pack.at[side, :, pl.ds(ROWS - REACH, REACH)], land.at[side, :, pl.ds(EXT - REACH, REACH)], self_sem.at[side]
        )

    raw_low = rows_raw(last, to_low, 0, 5, N)
    raw_fold = rows_raw(last, to_fold, 0, 0, N)
    raw_high = rows_raw(first, to_high, 5, 0, S)
    made_low = rows_made(last, to_low, 0, 5, N)
    made_fold = rows_made(last, to_fold, 0, 0, N)
    made_high = rows_made(first, to_high, 5, 0, S)
    strips_low = [strip(0, ROWS - REACH, PAD - REACH, 10, 12, NA), strip(1, ROWS - REACH, PAD - REACH, 11, 13, NB)]
    strips_fold = [strip(0, ROWS - REACH, EXT - REACH, 10, 10, NA), strip(1, ROWS - REACH, EXT - REACH, 11, 11, NB)]
    strips_high = [strip(0, 0, PAD + ROWS, 12, 10, SA), strip(1, 0, PAD + ROWS, 13, 11, SB)]
    strips_lon = [
        send(pack.at[0], land.at[0, :, own], 14, 14, W),
        send(pack.at[1], land.at[1, :, own], 15, 15, E),
    ]

    def start_all(copies):
        for copy in copies:
            copy.start()

    def start_raw(link):
        if link == N:
            pl.when(inner)(lambda: start_all(raw_low))
            pl.when(top)(lambda: start_all(raw_fold))
        else:
            start_all(raw_high)

    def start_made(link):
        if link in (W, E):
            strips_lon[link - W].start()
        elif link == N:
            pl.when(inner)(lambda: made_low.start())
            pl.when(top)(lambda: made_fold.start())
        elif link in (NA, NB):
            pl.when(inner)(lambda: strips_low[link - NA].start())
            pl.when(top)(lambda: strips_fold[link - NA].start())
        elif link == S:
            made_high.start()
        else:
            strips_high[link - SA].start()

    count = sum(jnp.where(g, 1, 0) for g in greeted)
    pl.when(count > 0)(lambda: pl.semaphore_wait(barrier, count))
    for link in range(8):

        @pl.when(greeted[link])
        def _(link=link):
            pl.semaphore_signal(ready.at[reverse[link]], inc=1, device_id=partner[link], device_id_type=MESH)

    for link in (N, S):
        pl.when(greeted[link])(lambda link=link: start_raw(link))

    for copy in loads:
        copy.wait()
    made[0] = mask_in[...].astype(jnp.float32)
    made[1] = wind_in[0].astype(jnp.float32)
    made[2] = wind_in[1].astype(jnp.float32)
    block = [vel_in.at[0], vel_in.at[1], sig_in.at[0], sig_in.at[1], sig_in.at[2], str_in]
    block += [made.at[0], made.at[1], made.at[2], cot_in.at[0], cot_in.at[1]]

    lanes = lane_ids((ROWS, COLS))
    for side in range(2):
        for plane in range(2):
            packed = None
            for field in range(NFLD):
                at_plane, begin_to, width = slot_of(field)
                if at_plane != plane:
                    continue
                begin = 0 if side == 0 else COLS - width
                value = block[field][...]
                shift = (begin_to - begin) % COLS
                if shift:
                    value = pltpu.roll(value, shift, 1)
                packed = value if packed is None else jnp.where(lanes < begin_to, packed, value)
            pack[side, plane] = packed

    for link in (N, S, NA, NB, SA, SB, W, E):
        pl.when(greeted[link])(lambda link=link: start_made(link))

    for side, is_self in ((0, self_a), (1, self_b)):
        pl.when(is_self)(lambda side=side: self_strip(side).start())

    for link in (W, E, N, NA, NB, S, SA, SB):

        @pl.when(greets[link])
        def _(link=link):
            pl.semaphore_wait(ready.at[link], 1)
            if link in (N, S):
                start_raw(link)
            start_made(link)

    for copy in strips_lon:
        copy.wait_recv()
    for copy in raw_high + [made_high]:
        copy.wait_recv()
    for side, is_self in ((0, self_a), (1, self_b)):
        pl.when(is_self)(lambda side=side: self_strip(side).wait())
        pl.when(jnp.logical_not(is_self))(lambda side=side: strips_high[side].wait_recv())

    @pl.when(has_south)
    def _():
        for copy in raw_low + [made_low] + strips_low:
            copy.wait_recv()
        for copy in raw_high + [made_high] + strips_high:
            copy.wait_send()

    for copy in raw_low + [made_low]:
        copy.wait_send()
    for side, is_self in ((0, self_a), (1, self_b)):
        pl.when(jnp.logical_not(is_self))(lambda side=side: strips_low[side].wait_send())
    for copy in strips_lon:
        copy.wait_send()


def gather_halos(lon_count, lat_count, *operands):
    f32 = jnp.float32
    hbm = pl.BlockSpec(memory_space=pltpu.HBM)
    return pl.pallas_call(
        partial(gather_kernel, lon_count, lat_count),
        out_shape=(
            jax.ShapeDtypeStruct((NFLD, EXT, COLS), f32),
            jax.ShapeDtypeStruct((2, 2, EXT, COLS), f32),
        ),
        in_specs=[hbm] * 6,
        out_specs=(hbm, hbm),
        scratch_shapes=[
            pltpu.VMEM((2, ROWS, COLS), jnp.bfloat16),
            pltpu.VMEM((ROWS, COLS), jnp.int32),
            pltpu.VMEM((2, ROWS, COLS), f32),
            pltpu.VMEM((3, ROWS, COLS), f32),
            pltpu.VMEM((ROWS, COLS), f32),
            pltpu.VMEM((2, ROWS, COLS), f32),
            pltpu.VMEM((3, ROWS, COLS), f32),
            pltpu.VMEM((2, 2, ROWS, COLS), f32),
            pltpu.SemaphoreType.DMA((6,)),
            pltpu.SemaphoreType.DMA((16,)),
            pltpu.SemaphoreType.DMA((16,)),
            pltpu.SemaphoreType.DMA((2,)),
            pltpu.SemaphoreType.REGULAR((8,)),
        ],
        compiler_params=pltpu.CompilerParams(
            collective_id=0, has_side_effects=True, vmem_limit_bytes=VMEM_LIMIT
        ),
    )(*operands)


TILE = 8


def tiles_for(reach):
    low = (PAD - reach) // TILE
    high = -(-(PAD + ROWS + reach) // TILE)
    return range(low * TILE, high * TILE, TILE)


def flip_tile(value):
    lane = lane_ids(value.shape)
    bit = 1
    while bit < COLS:
        value = jnp.where((lane & bit) != 0, pltpu.roll(value, bit, 1), pltpu.roll(value, COLS - bit, 1))
        bit *= 2
    row = lax.broadcasted_iota(jnp.int32, value.shape, 0)
    bit = 1
    while bit < TILE:
        value = jnp.where((row & bit) != 0, pltpu.roll(value, bit, 0), pltpu.roll(value, TILE - bit, 0))
        bit *= 2
    return value


def evp_kernel(
    lat_count,
    start,
    vel,
    sig,
    strength,
    wind,
    mask,
    cot,
    ext,
    land,
    final_vel,
    vel_grad,
    sig_grad,
    fld,
    state,
    turn,
    saved,
    back,
    strain,
    carry,
):
    band = lax.axis_index("lat")
    top = band == lat_count - 1
    bottom = band == 0
    shape = (TILE, COLS)
    lane = lane_ids(shape)
    first_lane = lane == 0
    last_lane = lane == COLS - 1
    west_half = lane < COLS // 2

    wind_f32 = wind[...].astype(jnp.float32)
    for r in range(0, EXT, TILE):
        rows = pl.ds(r, TILE)
        side = []
        for field in range(NFLD):
            plane, first, width = slot_of(field)
            a = land[0, plane, rows]
            b = land[1, plane, rows]
            shift_a = (-first) % COLS
            shift_b = (COLS - width - first) % COLS
            if shift_a:
                a = pltpu.roll(a, shift_a, 1)
            if shift_b:
                b = pltpu.roll(b, shift_b, 1)
            side.append(jnp.where(west_half, a, b))
        if PAD <= r < PAD + ROWS:
            mine = pl.ds(r - PAD, TILE)
            main = [vel[0, mine], vel[1, mine], sig[0, mine], sig[1, mine], sig[2, mine], strength[mine]]
            main += [mask[mine].astype(jnp.float32), wind_f32[0, r - PAD : r - PAD + TILE], wind_f32[1, r - PAD : r - PAD + TILE], cot[0, mine], cot[1, mine]]
        else:
            main = [ext[field, rows] for field in range(NFLD)]
        if r < PAD:
            main = [jnp.where(bottom, 0.0, x) for x in main]
            side = [jnp.where(bottom, 0.0, x) for x in side]
        for p, q in enumerate((main, side)):
            cover = q[6] * (1.0 / 1.5)
            q[2:7] = [
                0.125 * (q[2] + q[3]),
                0.125 * (q[2] - q[3]),
                0.25 * q[4],
                (1.0 / 16.0) * cover * q[5],
                cover,
            ]
            for field in range(NFLD):
                fld[field, p, rows] = q[field]

    @pl.when(top)
    def _():
        def one(i, _):
            odd = (i < 2) | (i >= 7)
            sign = jnp.where(odd, -1.0, 1.0)
            for plane in range(2):
                old = [fld[i, plane, pl.ds(PAD + ROWS + t * TILE, TILE)] for t in range(3)]
                for t in range(3):
                    fld[i, plane, pl.ds(PAD + ROWS + t * TILE, TILE)] = sign * flip_tile(old[2 - t])
            return 0

        lax.fori_loop(0, NFLD, one, 0)

    for r in range(0, EXT, TILE):
        rows = pl.ds(r, TILE)
        row = band * ROWS + (r - PAD) + lax.broadcasted_iota(jnp.int32, shape, 0)
        total = ROWS * lat_count
        row = jnp.where(row >= total, 2 * total - 1 - row, row).astype(jnp.float32)
        half_f = 0.6 * ((2.0 * row + 1.0) / total - 1.0)
        scale = 1.5 / (2.25 + half_f * half_f)
        for plane in range(2):
            cover = fld[6, plane, rows]
            turn[0, plane, rows] = cover * (1.5 * scale)
            turn[1, plane, rows] = cover * (half_f * scale)

    def at(ref, lead, plane, r):
        if r < 0:
            return pltpu.roll(ref[lead + (plane, pl.ds(0, TILE))], 1, 0)
        if r > EXT - TILE:
            return pltpu.roll(ref[lead + (plane, pl.ds(EXT - TILE, TILE))], TILE - 1, 0)
        return ref[lead + (plane, pl.ds(r, TILE))]

    def lat_diff(ref, lead, r):
        return [at(ref, lead, p, r + 1) - at(ref, lead, p, r - 1) for p in range(2)]

    def lon_diff(ref, lead, r):
        here = [at(ref, lead, p, r) for p in range(2)]
        east = [pltpu.roll(x, COLS - 1, 1) for x in here]
        west = [pltpu.roll(x, 1, 1) for x in here]
        return [
            jnp.where(last_lane, east[1 - p], east[p]) - jnp.where(first_lane, west[1 - p], west[p])
            for p in range(2)
        ]

    start_value = start[0].astype(jnp.float32)
    for k in range(NSUB):
        src = fld if k == 0 else state
        left = NSUB - 1 - k
        keep = set(tiles_for(2 * k + 1))
        for r in tiles_for(11 + 2 * left):
            rows = pl.ds(r, TILE)
            dux = lon_diff(src, (0,), r)
            dvx = lon_diff(src, (1,), r)
            duy = lat_diff(src, (0,), r)
            dvy = lat_diff(src, (1,), r)
            for p in range(2):
                div = dux[p] + dvy[p]
                ten = dux[p] - dvy[p]
                she = duy[p] + dvx[p]
                inv = lax.rsqrt(div * div + 0.25 * (ten * ten + she * she) + 1.0)
                part = fld[5, p, rows]
                div = div * inv
                inv4 = 0.25 * inv
                ten = ten * inv4
                she = she * inv4
                if r in keep:
                    saved[k, 0, p, rows] = div
                    saved[k, 1, p, rows] = ten
                    saved[k, 2, p, rows] = she
                    saved[k, 3, p, rows] = part * inv
                cover = fld[6, p, rows]
                pull = div - 1.0
                state[2, p, rows] = cover * src[2, p, rows] + part * (pull + ten)
                state[3, p, rows] = cover * src[3, p, rows] + part * (pull - ten)
                state[4, p, rows] = cover * src[4, p, rows] + part * she
        weight = 0.5 * ((start_value + (k + 1)) / EVP_TOTAL)
        for r in tiles_for(0 if left == 0 else 10 + 2 * left):
            rows = pl.ds(r, TILE)
            dxx = lon_diff(state, (2,), r)
            dxy = lon_diff(state, (4,), r)
            dyx = lat_diff(state, (4,), r)
            dyy = lat_diff(state, (3,), r)
            for p in range(2):
                ru = src[0, p, rows] + (dxx[p] + dyx[p]) + weight * fld[7, p, rows]
                rv = src[1, p, rows] + (dxy[p] + dyy[p]) + weight * fld[8, p, rows]
                ca = turn[0, p, rows]
                cb = turn[1, p, rows]
                un = ca * ru + cb * rv
                vn = ca * rv - cb * ru
                if left == 0:
                    if p == 0:
                        final_vel[0, pl.ds(r - PAD, TILE)] = un
                        final_vel[1, pl.ds(r - PAD, TILE)] = vn
                else:
                    state[0, p, rows] = un
                    state[1, p, rows] = vn

    for r in tiles_for(BACK):
        rows = pl.ds(r, TILE)
        for p in range(2):
            gu = fld[9, p, rows]
            gv = fld[10, p, rows]
            ca = turn[0, p, rows]
            cb = turn[1, p, rows]
            back[0, p, rows] = ca * gu - cb * gv
            back[1, p, rows] = cb * gu + ca * gv

    for k in reversed(range(NSUB)):
        for r in tiles_for(2 * k + 1):
            rows = pl.ds(r, TILE)
            dux = lon_diff(back, (0,), r)
            dvx = lon_diff(back, (1,), r)
            duy = lat_diff(back, (0,), r)
            dvy = lat_diff(back, (1,), r)
            for p in range(2):
                gx = -dux[p]
                gy = -dvy[p]
                gz = -(duy[p] + dvx[p])
                if k < NSUB - 1:
                    gx = carry[0, p, rows] + gx
                    gy = carry[1, p, rows] + gy
                    gz = carry[2, p, rows] + gz
                both = gx + gy
                apart = gx - gy
                cover = fld[6, p, rows]
                if k > 0:
                    carry[0, p, rows] = cover * gx
                    carry[1, p, rows] = cover * gy
                    carry[2, p, rows] = cover * gz
                elif p == 0 and PAD <= r < PAD + ROWS:
                    out = pl.ds(r - PAD, TILE)
                    c8 = 0.125 * cover
                    sig_grad[0, out] = c8 * both
                    sig_grad[1, out] = c8 * apart
                    sig_grad[2, out] = (0.25 * cover) * gz
                div = saved[k, 0, p, rows]
                ten = saved[k, 1, p, rows]
                she = saved[k, 2, p, rows]
                part = saved[k, 3, p, rows]
                along = both * div + apart * ten + gz * she
                g_div = part * (both - along * div)
                g_ten = part * (0.25 * apart - along * ten)
                strain[0, p, rows] = g_div + g_ten
                strain[1, p, rows] = g_div - g_ten
                strain[2, p, rows] = part * (0.25 * gz - along * she)
        for r in tiles_for(2 * k):
            rows = pl.ds(r, TILE)
            dax = lon_diff(strain, (0,), r)
            dsx = lon_diff(strain, (2,), r)
            dsy = lat_diff(strain, (2,), r)
            dby = lat_diff(strain, (1,), r)
            for p in range(2):
                gu = back[0, p, rows] - (dax[p] + dsy[p])
                gv = back[1, p, rows] - (dsx[p] + dby[p])
                if k > 0:
                    ca = turn[0, p, rows]
                    cb = turn[1, p, rows]
                    back[0, p, rows] = ca * gu - cb * gv
                    back[1, p, rows] = cb * gu + ca * gv
                elif p == 0:
                    vel_grad[0, pl.ds(r - PAD, TILE)] = gu
                    vel_grad[1, pl.ds(r - PAD, TILE)] = gv


def evp_and_adjoint(lat_count, start, *operands):
    f32 = jnp.float32
    vmem = pl.BlockSpec(memory_space=pltpu.VMEM)
    return pl.pallas_call(
        partial(evp_kernel, lat_count),
        out_shape=(
            jax.ShapeDtypeStruct((2, ROWS, COLS), f32),
            jax.ShapeDtypeStruct((2, ROWS, COLS), f32),
            jax.ShapeDtypeStruct((3, ROWS, COLS), f32),
        ),
        in_specs=[pl.BlockSpec(memory_space=pltpu.SMEM)] + [vmem] * 8,
        out_specs=(vmem, vmem, vmem),
        scratch_shapes=[
            pltpu.VMEM((NFLD, 2, EXT, COLS), f32),
            pltpu.VMEM((5, 2, EXT, COLS), f32),
            pltpu.VMEM((2, 2, EXT, COLS), f32),
            pltpu.VMEM((NSUB, 4, 2, EXT, COLS), f32),
            pltpu.VMEM((2, 2, EXT, COLS), f32),
            pltpu.VMEM((3, 2, EXT, COLS), f32),
            pltpu.VMEM((3, 2, EXT, COLS), f32),
        ],
        compiler_params=pltpu.CompilerParams(vmem_limit_bytes=VMEM_LIMIT),
    )(start, *operands)


def shards(lon_count, lat_count, velocity, stress, strength, wind_stress, ice_mask, start_step, velocity_cotangent):
    block = (velocity, stress, strength, wind_stress, ice_mask, velocity_cotangent)
    halos = gather_halos(lon_count, lat_count, *block)
    return evp_and_adjoint(lat_count, start_step, *block, *halos)


def solution(mesh):
    placed = (
        P(None, "lat", "lon"),
        P(None, "lat", "lon"),
        P("lat", "lon"),
        P(None, "lat", "lon"),
        P("lat", "lon"),
        P(),
        P(None, "lat", "lon"),
    )
    return jax.shard_map(
        partial(shards, mesh.shape["lon"], mesh.shape["lat"]),
        mesh=mesh,
        in_specs=placed,
        out_specs=(P(None, "lat", "lon"), P(None, "lat", "lon"), P(None, "lat", "lon")),
        check_vma=False,
    )
```

```python
from functools import partial

import jax
import jax.numpy as jnp
from jax import lax
from jax.experimental import pallas as pl
from jax.experimental.pallas import tpu as pltpu
from jax.sharding import PartitionSpec as P

NSUB = 6
EVP_TOTAL = 120
MESH = pl.DeviceIdType.MESH
VMEM_LIMIT = 60 * 1024 * 1024

ROWS = 48
COLS = 128
PAD = 24
EXT = ROWS + 2 * PAD
REACH = 22
BACK = 12
NFLD = 11
NMAIN = 9
SLOT = 24

ODD_FIELDS = (0, 1, 7, 8, 9, 10)


NEAR = 8
FAR = REACH - NEAR
FAR_SLOT = REACH - NEAR - 1
WIDE = ROWS + 2 * NEAR


def slot_of(field):
    if field < 5:
        return 0, SLOT * field, SLOT
    if field < NMAIN:
        return 1, SLOT * (field - 5), SLOT
    return 1, 4 * SLOT + BACK * (field - NMAIN), BACK


def far_slot_of(field):
    if field < NMAIN:
        return FAR_SLOT * field, FAR_SLOT
    return FAR_SLOT * NMAIN + (BACK - NEAR) * (field - NMAIN), BACK - NEAR


def strips(block, slots, side, shape):
    lanes = lane_ids(shape)
    packed = None
    for value, (to, width) in zip(block, slots):
        shift = (to - (0 if side == 0 else COLS - width)) % COLS
        if shift:
            value = pltpu.roll(value, shift, 1)
        packed = value if packed is None else jnp.where(lanes < to, packed, value)
    return packed


def unstrip(west, east, to, width):
    shift_a = (-to) % COLS
    shift_b = (COLS - width - to) % COLS
    if shift_a:
        west = pltpu.roll(west, shift_a, 1)
    if shift_b:
        east = pltpu.roll(east, shift_b, 1)
    return jnp.where(lane_ids(west.shape) < COLS // 2, west, east)


def lane_ids(shape):
    return lax.broadcasted_iota(jnp.int32, shape, len(shape) - 1)


def start_order(lon, lat):
    y = lax.div(lon, 8)
    z_low = lax.rem(lax.div(lon, 2), 4)
    x = lax.div(lat, 4)
    z_high = lax.rem(lat, 4)
    early_half = z_high < 2
    base = jnp.where(early_half, 44 * z_high, 96 - 4 * z_high)
    step = jnp.where(early_half, 13, 4)
    return 1024 * (7 * x + 7 * y + base + step * z_low) + 32 * lat + lon


def gather_kernel(
    lon_count,
    lat_count,
    vel,
    sig,
    strength,
    wind,
    mask,
    cot,
    ext,
    land,
    far,
    wind_in,
    mask_in,
    vel_in,
    sig_in,
    str_in,
    cot_in,
    made,
    pack,
    far_pack,
    local_sem,
    send_sem,
    recv_sem,
    self_sem,
    ready,
):
    lon = lax.axis_index("lon")
    lat = lax.axis_index("lat")
    top = lat == lat_count - 1
    inner = jnp.logical_not(top)
    has_south = lat > 0
    west = lax.rem(lon + lon_count - 1, lon_count)
    east = lax.rem(lon + 1, lon_count)
    up = jnp.where(top, lat, lat + 1)
    down = jnp.where(has_south, lat - 1, lat)
    north_lon = jnp.where(top, lon_count - 1 - lon, lon)
    north_a = jnp.where(top, lax.rem(lon_count - lon, lon_count), west)
    north_b = jnp.where(top, lax.rem(2 * lon_count - 2 - lon, lon_count), east)
    self_a = jnp.logical_and(top, north_a == lon)
    self_b = jnp.logical_and(top, north_b == lon)
    always = lat >= 0

    W, E, N, NA, NB, S, SA, SB = range(8)
    partner = [
        (west, lat),
        (east, lat),
        (north_lon, up),
        (north_a, up),
        (north_b, up),
        (lon, down),
        (west, down),
        (east, down),
    ]
    there = [always, always, always, jnp.logical_not(self_a), jnp.logical_not(self_b), has_south, has_south, has_south]
    reverse = [
        E,
        W,
        jnp.where(top, N, S),
        jnp.where(top, NA, SB),
        jnp.where(top, NB, SA),
        N,
        NB,
        NA,
    ]
    mine = start_order(lon, lat)
    later = [start_order(*p) > mine for p in partner]
    greets = [jnp.logical_and(t, l) for t, l in zip(there, later)]
    greeted = [jnp.logical_and(t, jnp.logical_not(l)) for t, l in zip(there, later)]

    barrier = pltpu.get_barrier_semaphore()
    for link in range(8):

        @pl.when(greets[link])
        def _(link=link):
            pl.semaphore_signal(barrier, inc=1, device_id=partner[link], device_id_type=MESH)

    own = pl.ds(PAD, ROWS)
    loads = [
        pltpu.make_async_copy(wind, wind_in, local_sem.at[0]),
        pltpu.make_async_copy(mask, mask_in, local_sem.at[1]),
        pltpu.make_async_copy(vel, vel_in, local_sem.at[2]),
        pltpu.make_async_copy(sig, sig_in, local_sem.at[3]),
        pltpu.make_async_copy(strength, str_in, local_sem.at[4]),
        pltpu.make_async_copy(cot, cot_in, local_sem.at[5]),
    ]
    for copy in loads:
        copy.start()

    def send(src, dst, slot, sem, link):
        return pltpu.make_async_remote_copy(
            src_ref=src,
            dst_ref=dst,
            send_sem=send_sem.at[slot],
            recv_sem=recv_sem.at[sem],
            device_id=partner[link],
            device_id_type=MESH,
        )

    def rows_raw(row_of, to_of, slot, sem, link):
        return [
            send(arg.at[index + (pl.ds(row_of(n), n),)], ext.at[to + (pl.ds(to_of(n), n),)], slot + i, sem + i, link)
            for i, (arg, index, to, n) in enumerate(
                (
                    (vel, (slice(None),), (pl.ds(0, 2),), REACH),
                    (sig, (slice(None),), (pl.ds(2, 3),), REACH - 1),
                    (strength, (), (5,), REACH - 1),
                    (cot, (slice(None),), (pl.ds(NMAIN, 2),), BACK),
                )
            )
        ]

    def rows_made(row_of, to_of, slot, sem, link):
        n, m = REACH - 1, REACH - 2
        return [
            send(made.at[0, pl.ds(row_of(n), n)], ext.at[6, pl.ds(to_of(n), n)], slot + 4, sem + 4, link),
            send(made.at[pl.ds(1, 2), pl.ds(row_of(m), m)], ext.at[pl.ds(7, 2), pl.ds(to_of(m), m)], slot + 5, sem + 5, link),
        ]

    last = lambda n: ROWS - n
    to_low = lambda n: PAD - n
    to_fold = lambda n: EXT - n
    first = lambda n: 0
    to_high = lambda n: PAD + ROWS

    def corner(side, row, to, far_row, far_to, slot, sem, link):
        return [
            send(pack.at[side, :, pl.ds(row, NEAR)], land.at[side, :, pl.ds(to, NEAR)], slot, sem, link),
            send(far_pack.at[side, pl.ds(far_row, FAR)], far.at[side, pl.ds(far_to, FAR)], slot + 1, sem + 1, link),
        ]

    def self_corner(side):
        return [
            pltpu.make_async_copy(
                pack.at[side, :, pl.ds(ROWS - NEAR, NEAR)], land.at[side, :, pl.ds(NEAR + ROWS, NEAR)], self_sem.at[2 * side]
            ),
            pltpu.make_async_copy(
                far_pack.at[side, pl.ds(ROWS - REACH, FAR)], far.at[side, pl.ds(PAD - NEAR + 2, FAR)], self_sem.at[2 * side + 1]
            ),
        ]

    raw_low = rows_raw(last, to_low, 0, 6, N)
    raw_fold = rows_raw(last, to_fold, 0, 0, N)
    raw_high = rows_raw(first, to_high, 6, 0, S)
    made_low = rows_made(last, to_low, 0, 6, N)
    made_fold = rows_made(last, to_fold, 0, 0, N)
    made_high = rows_made(first, to_high, 6, 0, S)
    far_low, far_high = PAD - REACH, PAD - NEAR
    corners_low = [corner(i, ROWS - NEAR, 0, ROWS - REACH, far_low, 12 + 2 * i, 16 + 2 * i, NA + i) for i in range(2)]
    corners_fold = [
        corner(i, ROWS - NEAR, NEAR + ROWS, ROWS - REACH, far_high + 2, 12 + 2 * i, 12 + 2 * i, NA + i) for i in range(2)
    ]
    corners_high = [corner(i, 0, NEAR + ROWS, NEAR, far_high, 16 + 2 * i, 12 + 2 * i, SA + i) for i in range(2)]
    strips_lon = [
        send(pack.at[0], land.at[0, :, pl.ds(NEAR, ROWS)], 20, 20, W),
        send(pack.at[1], land.at[1, :, pl.ds(NEAR, ROWS)], 21, 21, E),
    ]

    def start_all(copies):
        for copy in copies:
            copy.start()

    def start_rows(link, part):
        def pick(raw, made_rows):
            return raw[:1] if part == 0 else raw[1:3] + made_rows + raw[3:]

        if link == N:
            pl.when(inner)(lambda: start_all(pick(raw_low, made_low)))
            pl.when(top)(lambda: start_all(pick(raw_fold, made_fold)))
        else:
            start_all(pick(raw_high, made_high))

    def start_strips(link):
        if link in (W, E):
            strips_lon[link - W].start()
        elif link in (NA, NB):
            pl.when(inner)(lambda: start_all(corners_low[link - NA]))
            pl.when(top)(lambda: start_all(corners_fold[link - NA]))
        else:
            start_all(corners_high[link - SA])

    count = sum(jnp.where(g, 1, 0) for g in greeted)
    pl.when(count > 0)(lambda: pl.semaphore_wait(barrier, count))
    for link in range(8):

        @pl.when(greeted[link])
        def _(link=link):
            pl.semaphore_signal(ready.at[reverse[link]], inc=1, device_id=partner[link], device_id_type=MESH)

    for link in (N, S):
        pl.when(greeted[link])(lambda link=link: start_rows(link, 0))

    for copy in loads:
        copy.wait()
    made[0] = mask_in[...].astype(jnp.float32)
    made[1] = wind_in[0].astype(jnp.float32)
    made[2] = wind_in[1].astype(jnp.float32)
    block = [vel_in.at[0], vel_in.at[1], sig_in.at[0], sig_in.at[1], sig_in.at[2], str_in]
    block += [made.at[0], made.at[1], made.at[2], cot_in.at[0], cot_in.at[1]]

    values = [ref[...] for ref in block]
    for side in range(2):
        for plane in range(2):
            at = [f for f in range(NFLD) if slot_of(f)[0] == plane]
            pack[side, plane] = strips([values[f] for f in at], [slot_of(f)[1:] for f in at], side, (ROWS, COLS))
        inner_rows = slice(NEAR, ROWS - NEAR)
        far_pack[side, NEAR : ROWS - NEAR] = strips(
            [v[inner_rows] for v in values], [far_slot_of(f) for f in range(NFLD)], side, (ROWS - 2 * NEAR, COLS)
        )

    for link in (NA, NB, SA, SB, W, E):
        pl.when(greeted[link])(lambda link=link: start_strips(link))
    for link in (N, S):
        pl.when(greeted[link])(lambda link=link: start_rows(link, 1))

    for side, is_self in ((0, self_a), (1, self_b)):
        pl.when(is_self)(lambda side=side: start_all(self_corner(side)))

    for link, when in (
        [(link, always) for link in (W, E)]
        + [(link, inner) for link in (N, NA, NB)]
        + [(link, always) for link in (S, SA, SB)]
        + [(link, top) for link in (N, NA, NB)]
    ):

        @pl.when(jnp.logical_and(greets[link], when))
        def _(link=link):
            pl.semaphore_wait(ready.at[link], 1)
            if link in (N, S):
                start_rows(link, 0)
                start_rows(link, 1)
            else:
                start_strips(link)

    def received(copies):
        for copy in copies:
            copy.wait_recv()

    def sent(copies):
        for copy in copies:
            copy.wait_send()

    received(strips_lon)
    received(raw_high + made_high)
    for side, is_self in ((0, self_a), (1, self_b)):

        @pl.when(is_self)
        def _(side=side):
            for copy in self_corner(side):
                copy.wait()

        @pl.when(jnp.logical_not(is_self))
        def _(side=side):
            received(corners_high[side])
            sent(corners_low[side])

    @pl.when(has_south)
    def _():
        received(raw_low + made_low + corners_low[0] + corners_low[1])
        sent(raw_high + made_high + corners_high[0] + corners_high[1])

    sent(raw_low + made_low)
    sent(strips_lon)


def gather_halos(lon_count, lat_count, *operands):
    f32 = jnp.float32
    hbm = pl.BlockSpec(memory_space=pltpu.HBM)
    return pl.pallas_call(
        partial(gather_kernel, lon_count, lat_count),
        out_shape=(
            jax.ShapeDtypeStruct((NFLD, EXT, COLS), f32),
            jax.ShapeDtypeStruct((2, 2, WIDE, COLS), f32),
            jax.ShapeDtypeStruct((2, 2 * (PAD - NEAR), COLS), f32),
        ),
        in_specs=[hbm] * 6,
        out_specs=(hbm, hbm, hbm),
        scratch_shapes=[
            pltpu.VMEM((2, ROWS, COLS), jnp.bfloat16),
            pltpu.VMEM((ROWS, COLS), jnp.int32),
            pltpu.VMEM((2, ROWS, COLS), f32),
            pltpu.VMEM((3, ROWS, COLS), f32),
            pltpu.VMEM((ROWS, COLS), f32),
            pltpu.VMEM((2, ROWS, COLS), f32),
            pltpu.VMEM((3, ROWS, COLS), f32),
            pltpu.VMEM((2, 2, ROWS, COLS), f32),
            pltpu.VMEM((2, ROWS, COLS), f32),
            pltpu.SemaphoreType.DMA((6,)),
            pltpu.SemaphoreType.DMA((22,)),
            pltpu.SemaphoreType.DMA((22,)),
            pltpu.SemaphoreType.DMA((4,)),
            pltpu.SemaphoreType.REGULAR((8,)),
        ],
        compiler_params=pltpu.CompilerParams(
            collective_id=0, has_side_effects=True, vmem_limit_bytes=VMEM_LIMIT
        ),
    )(*operands)


TILE = 8


def tiles_for(reach):
    low = (PAD - reach) // TILE
    high = -(-(PAD + ROWS + reach) // TILE)
    return range(low * TILE, high * TILE, TILE)


def flip_tile(value):
    value = jnp.take_along_axis(value, COLS - 1 - lane_ids(value.shape), axis=1)
    row = lax.broadcasted_iota(jnp.int32, value.shape, 0)
    return jnp.take_along_axis(value, TILE - 1 - row, axis=0)


def evp_kernel(
    lat_count,
    start,
    vel,
    sig,
    strength,
    wind,
    mask,
    cot,
    ext,
    land,
    far,
    final_vel,
    vel_grad,
    sig_grad,
    fld,
    state,
    turn,
    saved,
    back,
    strain,
    carry,
):
    band = lax.axis_index("lat")
    top = band == lat_count - 1
    bottom = band == 0
    shape = (TILE, COLS)
    lane = lane_ids(shape)
    first_lane = lane == 0
    last_lane = lane == COLS - 1

    wind_f32 = wind[...].astype(jnp.float32)
    for r in range(0, EXT, TILE):
        rows = pl.ds(r, TILE)
        side = []
        for field in range(NFLD):
            if PAD - NEAR <= r < PAD + ROWS + NEAR:
                plane, to, width = slot_of(field)
                near = pl.ds(r - PAD + NEAR, TILE)
                side.append(unstrip(land[0, plane, near], land[1, plane, near], to, width))
            else:
                to, width = far_slot_of(field)
                beyond = pl.ds(r if r < PAD else r - ROWS - 2 * NEAR, TILE)
                side.append(unstrip(far[0, beyond], far[1, beyond], to, width))
        if PAD <= r < PAD + ROWS:
            mine = pl.ds(r - PAD, TILE)
            main = [vel[0, mine], vel[1, mine], sig[0, mine], sig[1, mine], sig[2, mine], strength[mine]]
            main += [mask[mine].astype(jnp.float32), wind_f32[0, r - PAD : r - PAD + TILE], wind_f32[1, r - PAD : r - PAD + TILE], cot[0, mine], cot[1, mine]]
        else:
            main = [ext[field, rows] for field in range(NFLD)]
        if r < PAD:
            main = [jnp.where(bottom, 0.0, x) for x in main]
            side = [jnp.where(bottom, 0.0, x) for x in side]
        for p, q in enumerate((main, side)):
            cover = q[6] * (1.0 / 1.5)
            q[2:7] = [
                0.125 * (q[2] + q[3]),
                0.125 * (q[2] - q[3]),
                0.25 * q[4],
                (1.0 / 16.0) * cover * q[5],
                cover,
            ]
            for field in range(NFLD):
                fld[field, p, rows] = q[field]

    @pl.when(top)
    def _():
        def one(i, _):
            odd = (i < 2) | (i >= 7)
            sign = jnp.where(odd, -1.0, 1.0)
            for plane in range(2):
                old = [fld[i, plane, pl.ds(PAD + ROWS + t * TILE, TILE)] for t in range(3)]
                order = (2, 1, 0) if plane == 0 else (0, 2, 1)
                for t in range(3):
                    fld[i, plane, pl.ds(PAD + ROWS + t * TILE, TILE)] = sign * flip_tile(old[order[t]])
            return 0

        lax.fori_loop(0, NFLD, one, 0)

    for r in range(0, EXT, TILE):
        rows = pl.ds(r, TILE)
        row = band * ROWS + (r - PAD) + lax.broadcasted_iota(jnp.int32, shape, 0)
        total = ROWS * lat_count
        row = jnp.where(row >= total, 2 * total - 1 - row, row).astype(jnp.float32)
        half_f = 0.6 * ((2.0 * row + 1.0) / total - 1.0)
        scale = 1.5 / (2.25 + half_f * half_f)
        for plane in range(2):
            cover = fld[6, plane, rows]
            turn[0, plane, rows] = cover * (1.5 * scale)
            turn[1, plane, rows] = cover * (half_f * scale)

    def at(ref, lead, plane, r):
        if r < 0:
            return pltpu.roll(ref[lead + (plane, pl.ds(0, TILE))], 1, 0)
        if r > EXT - TILE:
            return pltpu.roll(ref[lead + (plane, pl.ds(EXT - TILE, TILE))], TILE - 1, 0)
        return ref[lead + (plane, pl.ds(r, TILE))]

    def lat_diff(ref, lead, r):
        return [at(ref, lead, p, r + 1) - at(ref, lead, p, r - 1) for p in range(2)]

    def lon_diff(ref, lead, r):
        here = [at(ref, lead, p, r) for p in range(2)]
        east = [pltpu.roll(x, COLS - 1, 1) for x in here]
        west = [pltpu.roll(x, 1, 1) for x in here]
        return [
            jnp.where(last_lane, east[1 - p], east[p]) - jnp.where(first_lane, west[1 - p], west[p])
            for p in range(2)
        ]

    start_value = start[0].astype(jnp.float32)
    for k in range(NSUB):
        src = fld if k == 0 else state
        left = NSUB - 1 - k
        keep = set(tiles_for(2 * k + 1))
        for r in tiles_for(11 + 2 * left):
            rows = pl.ds(r, TILE)
            dux = lon_diff(src, (0,), r)
            dvx = lon_diff(src, (1,), r)
            duy = lat_diff(src, (0,), r)
            dvy = lat_diff(src, (1,), r)
            for p in range(2):
                div = dux[p] + dvy[p]
                ten = dux[p] - dvy[p]
                she = duy[p] + dvx[p]
                inv = lax.rsqrt(div * div + 0.25 * (ten * ten + she * she) + 1.0)
                part = fld[5, p, rows]
                div = div * inv
                inv4 = 0.25 * inv
                ten = ten * inv4
                she = she * inv4
                if r in keep:
                    saved[k, 0, p, rows] = div
                    saved[k, 1, p, rows] = ten
                    saved[k, 2, p, rows] = she
                    saved[k, 3, p, rows] = part * inv
                cover = fld[6, p, rows]
                pull = div - 1.0
                state[2, p, rows] = cover * src[2, p, rows] + part * (pull + ten)
                state[3, p, rows] = cover * src[3, p, rows] + part * (pull - ten)
                state[4, p, rows] = cover * src[4, p, rows] + part * she
        weight = 0.5 * ((start_value + (k + 1)) / EVP_TOTAL)
        for r in tiles_for(0 if left == 0 else 10 + 2 * left):
            rows = pl.ds(r, TILE)
            dxx = lon_diff(state, (2,), r)
            dxy = lon_diff(state, (4,), r)
            dyx = lat_diff(state, (4,), r)
            dyy = lat_diff(state, (3,), r)
            for p in range(2):
                ru = src[0, p, rows] + (dxx[p] + dyx[p]) + weight * fld[7, p, rows]
                rv = src[1, p, rows] + (dxy[p] + dyy[p]) + weight * fld[8, p, rows]
                ca = turn[0, p, rows]
                cb = turn[1, p, rows]
                un = ca * ru + cb * rv
                vn = ca * rv - cb * ru
                if left == 0:
                    if p == 0:
                        final_vel[0, pl.ds(r - PAD, TILE)] = un
                        final_vel[1, pl.ds(r - PAD, TILE)] = vn
                else:
                    state[0, p, rows] = un
                    state[1, p, rows] = vn

    for r in tiles_for(BACK):
        rows = pl.ds(r, TILE)
        for p in range(2):
            gu = fld[9, p, rows]
            gv = fld[10, p, rows]
            ca = turn[0, p, rows]
            cb = turn[1, p, rows]
            back[0, p, rows] = ca * gu - cb * gv
            back[1, p, rows] = cb * gu + ca * gv

    for k in reversed(range(NSUB)):
        for r in tiles_for(2 * k + 1):
            rows = pl.ds(r, TILE)
            dux = lon_diff(back, (0,), r)
            dvx = lon_diff(back, (1,), r)
            duy = lat_diff(back, (0,), r)
            dvy = lat_diff(back, (1,), r)
            for p in range(2):
                gx = -dux[p]
                gy = -dvy[p]
                gz = -(duy[p] + dvx[p])
                if k < NSUB - 1:
                    gx = carry[0, p, rows] + gx
                    gy = carry[1, p, rows] + gy
                    gz = carry[2, p, rows] + gz
                both = gx + gy
                apart = gx - gy
                cover = fld[6, p, rows]
                if k > 0:
                    carry[0, p, rows] = cover * gx
                    carry[1, p, rows] = cover * gy
                    carry[2, p, rows] = cover * gz
                elif p == 0 and PAD <= r < PAD + ROWS:
                    out = pl.ds(r - PAD, TILE)
                    c8 = 0.125 * cover
                    sig_grad[0, out] = c8 * both
                    sig_grad[1, out] = c8 * apart
                    sig_grad[2, out] = (0.25 * cover) * gz
                div = saved[k, 0, p, rows]
                ten = saved[k, 1, p, rows]
                she = saved[k, 2, p, rows]
                part = saved[k, 3, p, rows]
                along = both * div + apart * ten + gz * she
                g_div = part * (both - along * div)
                g_ten = part * (0.25 * apart - along * ten)
                strain[0, p, rows] = g_div + g_ten
                strain[1, p, rows] = g_div - g_ten
                strain[2, p, rows] = part * (0.25 * gz - along * she)
        for r in tiles_for(2 * k):
            rows = pl.ds(r, TILE)
            dax = lon_diff(strain, (0,), r)
            dsx = lon_diff(strain, (2,), r)
            dsy = lat_diff(strain, (2,), r)
            dby = lat_diff(strain, (1,), r)
            for p in range(2):
                gu = back[0, p, rows] - (dax[p] + dsy[p])
                gv = back[1, p, rows] - (dsx[p] + dby[p])
                if k > 0:
                    ca = turn[0, p, rows]
                    cb = turn[1, p, rows]
                    back[0, p, rows] = ca * gu - cb * gv
                    back[1, p, rows] = cb * gu + ca * gv
                elif p == 0:
                    vel_grad[0, pl.ds(r - PAD, TILE)] = gu
                    vel_grad[1, pl.ds(r - PAD, TILE)] = gv


def evp_and_adjoint(lat_count, start, *operands):
    f32 = jnp.float32
    vmem = pl.BlockSpec(memory_space=pltpu.VMEM)
    return pl.pallas_call(
        partial(evp_kernel, lat_count),
        out_shape=(
            jax.ShapeDtypeStruct((2, ROWS, COLS), f32),
            jax.ShapeDtypeStruct((2, ROWS, COLS), f32),
            jax.ShapeDtypeStruct((3, ROWS, COLS), f32),
        ),
        in_specs=[pl.BlockSpec(memory_space=pltpu.SMEM)] + [vmem] * 9,
        out_specs=(vmem, vmem, vmem),
        scratch_shapes=[
            pltpu.VMEM((NFLD, 2, EXT, COLS), f32),
            pltpu.VMEM((5, 2, EXT, COLS), f32),
            pltpu.VMEM((2, 2, EXT, COLS), f32),
            pltpu.VMEM((NSUB, 4, 2, EXT, COLS), f32),
            pltpu.VMEM((2, 2, EXT, COLS), f32),
            pltpu.VMEM((3, 2, EXT, COLS), f32),
            pltpu.VMEM((3, 2, EXT, COLS), f32),
        ],
        compiler_params=pltpu.CompilerParams(vmem_limit_bytes=VMEM_LIMIT),
    )(start, *operands)


def shards(lon_count, lat_count, velocity, stress, strength, wind_stress, ice_mask, start_step, velocity_cotangent):
    block = (velocity, stress, strength, wind_stress, ice_mask, velocity_cotangent)
    halos = gather_halos(lon_count, lat_count, *block)
    return evp_and_adjoint(lat_count, start_step, *block, *halos)


def solution(mesh):
    placed = (
        P(None, "lat", "lon"),
        P(None, "lat", "lon"),
        P("lat", "lon"),
        P(None, "lat", "lon"),
        P("lat", "lon"),
        P(),
        P(None, "lat", "lon"),
    )
    return jax.shard_map(
        partial(shards, mesh.shape["lon"], mesh.shape["lat"]),
        mesh=mesh,
        in_specs=placed,
        out_specs=(P(None, "lat", "lon"), P(None, "lat", "lon"), P(None, "lat", "lon")),
        check_vma=False,
    )
```

```python
from functools import partial

import jax
import jax.numpy as jnp
from jax import lax
from jax.experimental import pallas as pl
from jax.experimental.pallas import tpu as pltpu
from jax.sharding import PartitionSpec as P

NSUB = 6
EVP_TOTAL = 120
MESH = pl.DeviceIdType.MESH
VMEM_LIMIT = 32 * 1024 * 1024

ROWS = 48
COLS = 128
PAD = 24
EXT = ROWS + 2 * PAD
REACH = 22
BACK = 12
NFLD = 11
NMAIN = 9
SLOT = 24

ODD_FIELDS = (0, 1, 7, 8, 9, 10)


NEAR = 8
FAR = REACH - NEAR - 1
FAR_SLOT = REACH - NEAR - 1
WIDE = ROWS + 2 * NEAR


def slot_of(field):
    if field < 5:
        return 0, SLOT * field, SLOT
    if field < NMAIN:
        return 1, SLOT * (field - 5), SLOT
    return 1, 4 * SLOT + BACK * (field - NMAIN), BACK


def far_slot_of(field):
    if field < NMAIN:
        return FAR_SLOT * field, FAR_SLOT
    return FAR_SLOT * NMAIN + (BACK - NEAR) * (field - NMAIN), BACK - NEAR


def strips(block, slots, side, shape):
    lanes = lane_ids(shape)
    packed = None
    for value, (to, width) in zip(block, slots):
        shift = (to - (0 if side == 0 else COLS - width)) % COLS
        if shift:
            value = pltpu.roll(value, shift, 1)
        packed = value if packed is None else jnp.where(lanes < to, packed, value)
    return packed


def unstrip(west, east, to, width):
    shift_a = (-to) % COLS
    shift_b = (COLS - width - to) % COLS
    if shift_a:
        west = pltpu.roll(west, shift_a, 1)
    if shift_b:
        east = pltpu.roll(east, shift_b, 1)
    return jnp.where(lane_ids(west.shape) < COLS // 2, west, east)


def lane_ids(shape):
    return lax.broadcasted_iota(jnp.int32, shape, len(shape) - 1)


def digit(value, size, count):
    return sum(jnp.where(value >= size * i, 1, 0) for i in range(1, count))


def start_order(lon, lat):
    y = digit(lon, 8, 4)
    z_low = digit(lon - 8 * y, 2, 4)
    x = digit(lat, 4, 4)
    z_high = lat - 4 * x
    early_half = z_high < 2
    base = jnp.where(early_half, 44 * z_high, 96 - 4 * z_high)
    step = jnp.where(early_half, 13, 4)
    return 1024 * (7 * x + 7 * y + base + step * z_low) + 32 * lat + lon


def gather_kernel(
    lon_count,
    lat_count,
    vel,
    sig,
    strength,
    wind,
    mask,
    cot,
    ext,
    land,
    far,
    wind_in,
    mask_in,
    vel_in,
    sig_in,
    cot_in,
    made,
    pack,
    far_pack,
    local_sem,
    send_sem,
    recv_sem,
    self_sem,
    ready,
):
    lon = lax.axis_index("lon")
    lat = lax.axis_index("lat")
    top = lat == lat_count - 1
    inner = jnp.logical_not(top)
    has_south = lat > 0
    west = jnp.where(lon == 0, lon_count - 1, lon - 1)
    east = jnp.where(lon == lon_count - 1, 0, lon + 1)
    up = jnp.where(top, lat, lat + 1)
    down = jnp.where(has_south, lat - 1, lat)
    north_lon = jnp.where(top, lon_count - 1 - lon, lon)
    north_a = jnp.where(top, jnp.where(lon == 0, 0, lon_count - lon), west)
    north_b = jnp.where(top, lon_count - 2 - lon + jnp.where(lon == lon_count - 1, lon_count, 0), east)
    self_a = jnp.logical_and(top, north_a == lon)
    self_b = jnp.logical_and(top, north_b == lon)
    always = lat >= 0

    W, E, N, NA, NB, S, SA, SB = range(8)
    partner = [
        (west, lat),
        (east, lat),
        (north_lon, up),
        (north_a, up),
        (north_b, up),
        (lon, down),
        (west, down),
        (east, down),
    ]
    there = [always, always, always, jnp.logical_not(self_a), jnp.logical_not(self_b), has_south, has_south, has_south]
    reverse = [
        E,
        W,
        jnp.where(top, N, S),
        jnp.where(top, NA, SB),
        jnp.where(top, NB, SA),
        N,
        NB,
        NA,
    ]
    mine = start_order(lon, lat)
    plain = [(west, lat), (east, lat), (lon, up), (west, up), (east, up), (lon, down), (west, down), (east, down)]
    later = [start_order(*p) > mine for p in plain]
    folded = [jnp.logical_and(top, link in (N, NA, NB)) for link in range(8)]
    answers = [there[i] & jnp.logical_not(later[i]) & jnp.logical_not(folded[i]) for i in range(8)]
    awaits = [there[i] & later[i] & jnp.logical_not(folded[i]) for i in range(8)]
    greets = [there[i] & (later[i] | folded[i]) for i in range(8)]
    greeted = [there[i] & (jnp.logical_not(later[i]) | folded[i]) for i in range(8)]

    barrier = pltpu.get_barrier_semaphore()
    for link in range(8):

        @pl.when(greets[link])
        def _(link=link):
            pl.semaphore_signal(barrier, inc=1, device_id=partner[link], device_id_type=MESH)

    own = pl.ds(PAD, ROWS)
    loads = [
        pltpu.make_async_copy(wind, wind_in, local_sem.at[0]),
        pltpu.make_async_copy(mask, mask_in, local_sem.at[1]),
        pltpu.make_async_copy(vel, vel_in, local_sem.at[2]),
        pltpu.make_async_copy(sig, sig_in, local_sem.at[3]),
        pltpu.make_async_copy(strength, made.at[0], local_sem.at[4]),
        pltpu.make_async_copy(cot, cot_in, local_sem.at[5]),
    ]
    for copy in loads:
        copy.start()

    def send(src, dst, slot, sem, link):
        return pltpu.make_async_remote_copy(
            src_ref=src,
            dst_ref=dst,
            send_sem=send_sem.at[slot],
            recv_sem=recv_sem.at[sem],
            device_id=partner[link],
            device_id_type=MESH,
        )

    def rows_raw(row_of, to_of, slot, sem, link):
        return [
            send(arg.at[index + (pl.ds(row_of(n), n),)], ext.at[to + (pl.ds(to_of(n), n),)], slot + i, sem + i, link)
            for i, (arg, index, to, n) in enumerate(
                (
                    (vel, (slice(None),), (pl.ds(0, 2),), REACH),
                    (sig, (slice(None),), (pl.ds(2, 3),), REACH - 1),
                    (cot, (slice(None),), (pl.ds(NMAIN, 2),), BACK),
                )
            )
        ]

    def rows_made(row_of, to_of, slot, sem, link):
        n, m = REACH - 1, REACH - 2
        return [
            send(made.at[pl.ds(0, 2), pl.ds(row_of(n), n)], ext.at[pl.ds(5, 2), pl.ds(to_of(n), n)], slot + 3, sem + 3, link),
            send(made.at[pl.ds(2, 2), pl.ds(row_of(m), m)], ext.at[pl.ds(7, 2), pl.ds(to_of(m), m)], slot + 4, sem + 4, link),
        ]

    last = lambda n: ROWS - n
    to_low = lambda n: PAD - n
    to_fold = lambda n: EXT - n
    first = lambda n: 0
    to_high = lambda n: PAD + ROWS

    def corner(side, row, to, far_row, far_to, slot, sem, link):
        return [
            send(pack.at[side, :, pl.ds(row, NEAR)], land.at[side, :, pl.ds(to, NEAR)], slot, sem, link),
            send(far_pack.at[side, pl.ds(far_row, FAR)], far.at[side, pl.ds(far_to, FAR)], slot + 1, sem + 1, link),
        ]

    def self_corner(side):
        return [
            pltpu.make_async_copy(
                pack.at[side, :, pl.ds(ROWS - NEAR, NEAR)], land.at[side, :, pl.ds(NEAR + ROWS, NEAR)], self_sem.at[2 * side]
            ),
            pltpu.make_async_copy(
                far_pack.at[side, pl.ds(ROWS - REACH + 1, FAR)], far.at[side, pl.ds(PAD - NEAR + 3, FAR)], self_sem.at[2 * side + 1]
            ),
        ]

    raw_low = rows_raw(last, to_low, 0, 6, N)
    raw_fold = rows_raw(last, to_fold, 0, 0, N)
    raw_high = rows_raw(first, to_high, 6, 0, S)
    made_low = rows_made(last, to_low, 0, 6, N)
    made_fold = rows_made(last, to_fold, 0, 0, N)
    made_high = rows_made(first, to_high, 6, 0, S)
    far_low, far_high = PAD - REACH + 1, PAD - NEAR
    far_row = ROWS - REACH + 1
    corners_low = [corner(i, ROWS - NEAR, 0, far_row, far_low, 12 + 2 * i, 16 + 2 * i, NA + i) for i in range(2)]
    corners_fold = [
        corner(i, ROWS - NEAR, NEAR + ROWS, far_row, far_high + 3, 12 + 2 * i, 12 + 2 * i, NA + i) for i in range(2)
    ]
    corners_high = [corner(i, 0, NEAR + ROWS, NEAR, far_high, 16 + 2 * i, 12 + 2 * i, SA + i) for i in range(2)]
    strips_lon = [
        send(pack.at[0], land.at[0, :, pl.ds(NEAR, ROWS)], 20, 20, W),
        send(pack.at[1], land.at[1, :, pl.ds(NEAR, ROWS)], 21, 21, E),
    ]

    def start_all(copies):
        for copy in copies:
            copy.start()

    def start_rows(link, part):
        def pick(raw, made_rows):
            return (raw[:1], raw[1:2], made_rows + raw[2:])[part]

        if link == N:
            pl.when(inner)(lambda: start_all(pick(raw_low, made_low)))
            pl.when(top)(lambda: start_all(pick(raw_fold, made_fold)))
        else:
            start_all(pick(raw_high, made_high))

    def start_strips(link):
        if link in (W, E):
            strips_lon[link - W].start()
        elif link in (NA, NB):
            pl.when(inner)(lambda: start_all(corners_low[link - NA]))
            pl.when(top)(lambda: start_all(corners_fold[link - NA]))
        else:
            start_all(corners_high[link - SA])

    count = sum(jnp.where(g, 1, 0) for g in greeted)
    pl.when(count > 0)(lambda: pl.semaphore_wait(barrier, count))
    for link in range(8):

        @pl.when(answers[link])
        def _(link=link):
            pl.semaphore_signal(ready.at[reverse[link]], inc=1, device_id=partner[link], device_id_type=MESH)

    for link in (N, S):
        pl.when(greeted[link])(lambda link=link: start_rows(link, 0))

    for copy in loads:
        copy.wait()
    made[1] = mask_in[...].astype(jnp.float32)
    made[2] = wind_in[0].astype(jnp.float32)
    made[3] = wind_in[1].astype(jnp.float32)
    block = [vel_in.at[0], vel_in.at[1], sig_in.at[0], sig_in.at[1], sig_in.at[2]]
    block += [made.at[0], made.at[1], made.at[2], made.at[3], cot_in.at[0], cot_in.at[1]]

    values = [ref[...] for ref in block]
    for side in range(2):
        for plane in range(2):
            at = [f for f in range(NFLD) if slot_of(f)[0] == plane]
            pack[side, plane] = strips([values[f] for f in at], [slot_of(f)[1:] for f in at], side, (ROWS, COLS))
        inner_rows = slice(NEAR, ROWS - NEAR)
        far_pack[side, NEAR : ROWS - NEAR] = strips(
            [v[inner_rows] for v in values], [far_slot_of(f) for f in range(NFLD)], side, (ROWS - 2 * NEAR, COLS)
        )

    for link in (NA, NB, SA, SB, W, E):
        pl.when(greeted[link])(lambda link=link: start_strips(link))
    patient = top & (lon < lon_count // 2)
    for part in (1, 2):
        for link in (N, S):
            wait = patient if link == N else jnp.logical_not(always)
            pl.when(greeted[link] & jnp.logical_not(wait))(lambda link=link, part=part: start_rows(link, part))

    for side, is_self in ((0, self_a), (1, self_b)):
        pl.when(is_self)(lambda side=side: start_all(self_corner(side)))

    for link in (W, E, N, NA, NB, S, SA, SB):

        @pl.when(awaits[link])
        def _(link=link):
            pl.semaphore_wait(ready.at[link], 1)
            if link in (N, S):
                start_rows(link, 0)
                start_rows(link, 1)
                start_rows(link, 2)
            else:
                start_strips(link)

    for part in (1, 2):
        pl.when(patient)(lambda part=part: start_rows(N, part))

    def received(copies):
        for copy in copies:
            copy.wait_recv()

    def sent(copies):
        for copy in copies:
            copy.wait_send()

    received(strips_lon)
    received(raw_high + made_high)
    for side, is_self in ((0, self_a), (1, self_b)):

        @pl.when(is_self)
        def _(side=side):
            for copy in self_corner(side):
                copy.wait()

        @pl.when(jnp.logical_not(is_self))
        def _(side=side):
            received(corners_high[side])
            sent(corners_low[side])

    @pl.when(has_south)
    def _():
        received(raw_low + made_low + corners_low[0] + corners_low[1])
        sent(raw_high + made_high + corners_high[0] + corners_high[1])

    sent(raw_low + made_low)
    sent(strips_lon)


def gather_halos(lon_count, lat_count, *operands):
    f32 = jnp.float32
    anywhere = pl.BlockSpec(memory_space=pl.ANY)
    return pl.pallas_call(
        partial(gather_kernel, lon_count, lat_count),
        out_shape=(
            jax.ShapeDtypeStruct((NFLD, EXT, COLS), f32),
            jax.ShapeDtypeStruct((2, 2, WIDE, COLS), f32),
            jax.ShapeDtypeStruct((2, 2 * (PAD - NEAR), COLS), f32),
        ),
        in_specs=[pl.BlockSpec(memory_space=pltpu.HBM)] * 6,
        out_specs=(anywhere, anywhere, anywhere),
        scratch_shapes=[
            pltpu.VMEM((2, ROWS, COLS), jnp.bfloat16),
            pltpu.VMEM((ROWS, COLS), jnp.int32),
            pltpu.VMEM((2, ROWS, COLS), f32),
            pltpu.VMEM((3, ROWS, COLS), f32),
            pltpu.VMEM((2, ROWS, COLS), f32),
            pltpu.VMEM((4, ROWS, COLS), f32),
            pltpu.VMEM((2, 2, ROWS, COLS), f32),
            pltpu.VMEM((2, ROWS, COLS), f32),
            pltpu.SemaphoreType.DMA((6,)),
            pltpu.SemaphoreType.DMA((22,)),
            pltpu.SemaphoreType.DMA((22,)),
            pltpu.SemaphoreType.DMA((4,)),
            pltpu.SemaphoreType.REGULAR((8,)),
        ],
        compiler_params=pltpu.CompilerParams(
            collective_id=0, has_side_effects=True, vmem_limit_bytes=VMEM_LIMIT
        ),
    )(*operands)


TILE = 8


def tiles_for(reach):
    low = (PAD - reach) // TILE
    high = -(-(PAD + ROWS + reach) // TILE)
    return range(low * TILE, high * TILE, TILE)


def flip_tile(value):
    value = jnp.take_along_axis(value, COLS - 1 - lane_ids(value.shape), axis=1)
    row = lax.broadcasted_iota(jnp.int32, value.shape, 0)
    return jnp.take_along_axis(value, TILE - 1 - row, axis=0)


def evp_kernel(
    lat_count,
    start,
    vel,
    sig,
    strength,
    wind,
    mask,
    cot,
    ext,
    land,
    far,
    final_vel,
    vel_grad,
    sig_grad,
    fld,
    state,
    turn,
    saved,
    back,
    strain,
    carry,
):
    band = lax.axis_index("lat")
    top = band == lat_count - 1
    bottom = band == 0
    shape = (TILE, COLS)
    lane = lane_ids(shape)
    first_lane = lane == 0
    last_lane = lane == COLS - 1

    wind_f32 = wind[...].astype(jnp.float32)
    for r in range(0, EXT, TILE):
        rows = pl.ds(r, TILE)
        side = []
        for field in range(NFLD):
            if PAD - NEAR <= r < PAD + ROWS + NEAR:
                plane, to, width = slot_of(field)
                near = pl.ds(r - PAD + NEAR, TILE)
                side.append(unstrip(land[0, plane, near], land[1, plane, near], to, width))
            else:
                to, width = far_slot_of(field)
                beyond = pl.ds(r if r < PAD else r - ROWS - 2 * NEAR, TILE)
                side.append(unstrip(far[0, beyond], far[1, beyond], to, width))
        if PAD <= r < PAD + ROWS:
            mine = pl.ds(r - PAD, TILE)
            main = [vel[0, mine], vel[1, mine], sig[0, mine], sig[1, mine], sig[2, mine], strength[mine]]
            main += [mask[mine].astype(jnp.float32), wind_f32[0, r - PAD : r - PAD + TILE], wind_f32[1, r - PAD : r - PAD + TILE], cot[0, mine], cot[1, mine]]
        else:
            main = [ext[field, rows] for field in range(NFLD)]
        if r < PAD:
            main = [jnp.where(bottom, 0.0, x) for x in main]
            side = [jnp.where(bottom, 0.0, x) for x in side]
        for p, q in enumerate((main, side)):
            cover = q[6] * (1.0 / 1.5)
            q[2:7] = [
                0.125 * (q[2] + q[3]),
                0.125 * (q[2] - q[3]),
                0.25 * q[4],
                (1.0 / 16.0) * cover * q[5],
                cover,
            ]
            for field in range(NFLD):
                fld[field, p, rows] = q[field]

    @pl.when(top)
    def _():
        for field in range(NFLD):
            for plane in range(2):
                old = [fld[field, plane, pl.ds(PAD + ROWS + t * TILE, TILE)] for t in range(3)]
                order = (2, 1, 0) if plane == 0 else (0, 2, 1)
                for t in range(3):
                    new = flip_tile(old[order[t]])
                    fld[field, plane, pl.ds(PAD + ROWS + t * TILE, TILE)] = -new if field in ODD_FIELDS else new

    for r in range(0, EXT, TILE):
        rows = pl.ds(r, TILE)
        row = band * ROWS + (r - PAD) + lax.broadcasted_iota(jnp.int32, shape, 0)
        total = ROWS * lat_count
        row = jnp.where(row >= total, 2 * total - 1 - row, row).astype(jnp.float32)
        half_f = 0.6 * ((2.0 * row + 1.0) / total - 1.0)
        scale = 1.5 / (2.25 + half_f * half_f)
        for plane in range(2):
            cover = fld[6, plane, rows]
            turn[0, plane, rows] = cover * (1.5 * scale)
            turn[1, plane, rows] = cover * (half_f * scale)

    def at(ref, lead, plane, r):
        if r < 0:
            return pltpu.roll(ref[lead + (plane, pl.ds(0, TILE))], 1, 0)
        if r > EXT - TILE:
            return pltpu.roll(ref[lead + (plane, pl.ds(EXT - TILE, TILE))], TILE - 1, 0)
        return ref[lead + (plane, pl.ds(r, TILE))]

    def lat_diff(ref, lead, r):
        return [at(ref, lead, p, r + 1) - at(ref, lead, p, r - 1) for p in range(2)]

    def lon_diff(ref, lead, r):
        here = [at(ref, lead, p, r) for p in range(2)]
        east = [pltpu.roll(x, COLS - 1, 1) for x in here]
        west = [pltpu.roll(x, 1, 1) for x in here]
        return [
            jnp.where(last_lane, east[1 - p], east[p]) - jnp.where(first_lane, west[1 - p], west[p])
            for p in range(2)
        ]

    start_value = start[0].astype(jnp.float32)
    for k in range(NSUB):
        src = fld if k == 0 else state
        left = NSUB - 1 - k
        keep = set(tiles_for(2 * k + 1))
        for r in tiles_for(11 + 2 * left):
            rows = pl.ds(r, TILE)
            dux = lon_diff(src, (0,), r)
            dvx = lon_diff(src, (1,), r)
            duy = lat_diff(src, (0,), r)
            dvy = lat_diff(src, (1,), r)
            for p in range(2):
                div = dux[p] + dvy[p]
                ten = dux[p] - dvy[p]
                she = duy[p] + dvx[p]
                inv = lax.rsqrt(div * div + 0.25 * (ten * ten + she * she) + 1.0)
                part = fld[5, p, rows]
                div = div * inv
                inv4 = 0.25 * inv
                ten = ten * inv4
                she = she * inv4
                if r in keep:
                    saved[k, 0, p, rows] = div
                    saved[k, 1, p, rows] = ten
                    saved[k, 2, p, rows] = she
                    saved[k, 3, p, rows] = part * inv
                cover = fld[6, p, rows]
                pull = div - 1.0
                state[2, p, rows] = cover * src[2, p, rows] + part * (pull + ten)
                state[3, p, rows] = cover * src[3, p, rows] + part * (pull - ten)
                state[4, p, rows] = cover * src[4, p, rows] + part * she
        weight = 0.5 * ((start_value + (k + 1)) / EVP_TOTAL)
        for r in tiles_for(0 if left == 0 else 10 + 2 * left):
            rows = pl.ds(r, TILE)
            dxx = lon_diff(state, (2,), r)
            dxy = lon_diff(state, (4,), r)
            dyx = lat_diff(state, (4,), r)
            dyy = lat_diff(state, (3,), r)
            for p in range(2):
                ru = src[0, p, rows] + (dxx[p] + dyx[p]) + weight * fld[7, p, rows]
                rv = src[1, p, rows] + (dxy[p] + dyy[p]) + weight * fld[8, p, rows]
                ca = turn[0, p, rows]
                cb = turn[1, p, rows]
                un = ca * ru + cb * rv
                vn = ca * rv - cb * ru
                if left == 0:
                    if p == 0:
                        final_vel[0, pl.ds(r - PAD, TILE)] = un
                        final_vel[1, pl.ds(r - PAD, TILE)] = vn
                else:
                    state[0, p, rows] = un
                    state[1, p, rows] = vn

    for r in tiles_for(BACK):
        rows = pl.ds(r, TILE)
        for p in range(2):
            gu = fld[9, p, rows]
            gv = fld[10, p, rows]
            ca = turn[0, p, rows]
            cb = turn[1, p, rows]
            back[0, p, rows] = ca * gu - cb * gv
            back[1, p, rows] = cb * gu + ca * gv

    for k in reversed(range(NSUB)):
        for r in tiles_for(2 * k + 1):
            rows = pl.ds(r, TILE)
            dux = lon_diff(back, (0,), r)
            dvx = lon_diff(back, (1,), r)
            duy = lat_diff(back, (0,), r)
            dvy = lat_diff(back, (1,), r)
            for p in range(2):
                gx = -dux[p]
                gy = -dvy[p]
                gz = -(duy[p] + dvx[p])
                if k < NSUB - 1:
                    gx = carry[0, p, rows] + gx
                    gy = carry[1, p, rows] + gy
                    gz = carry[2, p, rows] + gz
                both = gx + gy
                apart = gx - gy
                cover = fld[6, p, rows]
                if k > 0:
                    carry[0, p, rows] = cover * gx
                    carry[1, p, rows] = cover * gy
                    carry[2, p, rows] = cover * gz
                elif p == 0 and PAD <= r < PAD + ROWS:
                    out = pl.ds(r - PAD, TILE)
                    c8 = 0.125 * cover
                    sig_grad[0, out] = c8 * both
                    sig_grad[1, out] = c8 * apart
                    sig_grad[2, out] = (0.25 * cover) * gz
                div = saved[k, 0, p, rows]
                ten = saved[k, 1, p, rows]
                she = saved[k, 2, p, rows]
                part = saved[k, 3, p, rows]
                along = both * div + apart * ten + gz * she
                g_div = part * (both - along * div)
                g_ten = part * (0.25 * apart - along * ten)
                strain[0, p, rows] = g_div + g_ten
                strain[1, p, rows] = g_div - g_ten
                strain[2, p, rows] = part * (0.25 * gz - along * she)
        for r in tiles_for(2 * k):
            rows = pl.ds(r, TILE)
            dax = lon_diff(strain, (0,), r)
            dsx = lon_diff(strain, (2,), r)
            dsy = lat_diff(strain, (2,), r)
            dby = lat_diff(strain, (1,), r)
            for p in range(2):
                gu = back[0, p, rows] - (dax[p] + dsy[p])
                gv = back[1, p, rows] - (dsx[p] + dby[p])
                if k > 0:
                    ca = turn[0, p, rows]
                    cb = turn[1, p, rows]
                    back[0, p, rows] = ca * gu - cb * gv
                    back[1, p, rows] = cb * gu + ca * gv
                elif p == 0:
                    vel_grad[0, pl.ds(r - PAD, TILE)] = gu
                    vel_grad[1, pl.ds(r - PAD, TILE)] = gv


def evp_and_adjoint(lat_count, start, *operands):
    f32 = jnp.float32
    vmem = pl.BlockSpec(memory_space=pltpu.VMEM)
    return pl.pallas_call(
        partial(evp_kernel, lat_count),
        out_shape=(
            jax.ShapeDtypeStruct((2, ROWS, COLS), f32),
            jax.ShapeDtypeStruct((2, ROWS, COLS), f32),
            jax.ShapeDtypeStruct((3, ROWS, COLS), f32),
        ),
        in_specs=[pl.BlockSpec(memory_space=pltpu.SMEM)] + [vmem] * 9,
        out_specs=(vmem, vmem, vmem),
        scratch_shapes=[
            pltpu.VMEM((NFLD, 2, EXT, COLS), f32),
            pltpu.VMEM((5, 2, EXT, COLS), f32),
            pltpu.VMEM((2, 2, EXT, COLS), f32),
            pltpu.VMEM((NSUB, 4, 2, EXT, COLS), f32),
            pltpu.VMEM((2, 2, EXT, COLS), f32),
            pltpu.VMEM((3, 2, EXT, COLS), f32),
            pltpu.VMEM((3, 2, EXT, COLS), f32),
        ],
        compiler_params=pltpu.CompilerParams(vmem_limit_bytes=VMEM_LIMIT),
    )(start, *operands)


def shards(lon_count, lat_count, velocity, stress, strength, wind_stress, ice_mask, start_step, velocity_cotangent):
    block = (velocity, stress, strength, wind_stress, ice_mask, velocity_cotangent)
    halos = gather_halos(lon_count, lat_count, *(pltpu.with_memory_space_constraint(x, pltpu.HBM) for x in block))
    return evp_and_adjoint(lat_count, start_step, *block, *halos)


def solution(mesh):
    placed = (
        P(None, "lat", "lon"),
        P(None, "lat", "lon"),
        P("lat", "lon"),
        P(None, "lat", "lon"),
        P("lat", "lon"),
        P(),
        P(None, "lat", "lon"),
    )
    return jax.shard_map(
        partial(shards, mesh.shape["lon"], mesh.shape["lat"]),
        mesh=mesh,
        in_specs=placed,
        out_specs=(P(None, "lat", "lon"), P(None, "lat", "lon"), P(None, "lat", "lon")),
        check_vma=False,
    )
```

```python
from functools import partial

import jax
import jax.numpy as jnp
from jax import lax
from jax.experimental import pallas as pl
from jax.experimental.pallas import tpu as pltpu
from jax.sharding import PartitionSpec as P

NSUB = 6
EVP_TOTAL = 120
MESH = pl.DeviceIdType.MESH
VMEM_LIMIT = 32 * 1024 * 1024

ROWS = 48
COLS = 128
PAD = 24
EXT = ROWS + 2 * PAD
REACH = 22
BACK = 12
TILE = 8
NFLD = 11
NMAIN = 9
SLOT = 24

ODD_FIELDS = (0, 1, 7, 8, 9, 10)


GROUP = 7


def slot_of(field):
    if field < 5:
        return 0, SLOT * field, SLOT
    if field < NMAIN:
        return 1, SLOT * (field - 5), SLOT
    return 1, 4 * SLOT + BACK * (field - NMAIN), BACK


def corner_width(field, row):
    return (REACH, REACH, *(REACH - 1,) * 5, REACH - 2, REACH - 2, BACK, BACK)[field] - row


def corner_slots():
    wide = [(0, field, corner_width(field, 1)) for field in range(NFLD)]
    narrow = [(2, field, corner_width(field, 15)) for field in range(NMAIN)]
    planes = [wide[:6] + narrow[2:3], wide[6:] + narrow[:2] + narrow[3:]]
    planes.append([(1, field, corner_width(field, 8)) for field in range(NFLD)])
    placed = []
    for plane in planes:
        to = 0
        placed.append([])
        for group, field, width in plane:
            placed[-1].append((group, field, to, width))
            to += width
        assert to <= COLS
    return placed


def corner_rows(end, group):
    return ROWS - TILE - GROUP * group if end == 0 else GROUP * group


def strips(block, slots, side, shape):
    lanes = lane_ids(shape)
    packed = None
    for value, (to, width) in zip(block, slots):
        shift = (to - (0 if side == 0 else COLS - width)) % COLS
        if shift:
            value = pltpu.roll(value, shift, 1)
        packed = value if packed is None else jnp.where(lanes < to, packed, value)
    return packed


def unstrip(west, east, to, width):
    shift_a = (-to) % COLS
    shift_b = (COLS - width - to) % COLS
    if shift_a:
        west = pltpu.roll(west, shift_a, 1)
    if shift_b:
        east = pltpu.roll(east, shift_b, 1)
    return jnp.where(lane_ids(west.shape) < COLS // 2, west, east)


def lane_ids(shape):
    return lax.broadcasted_iota(jnp.int32, shape, len(shape) - 1)


def digit(value, size, count):
    return sum(jnp.where(value >= size * i, 1, 0) for i in range(1, count))


def start_order(lon, lat):
    y = digit(lon, 8, 4)
    z_low = digit(lon - 8 * y, 2, 4)
    x = digit(lat, 4, 4)
    z_high = lat - 4 * x
    early_half = z_high < 2
    base = jnp.where(early_half, 44 * z_high, 96 - 4 * z_high)
    step = jnp.where(early_half, 13, 4)
    return 1024 * (7 * x + 7 * y + base + step * z_low) + 32 * lat + lon


def gather_kernel(
    lon_count,
    lat_count,
    vel,
    sig,
    strength,
    wind,
    mask,
    cot,
    ext,
    land,
    corners,
    wind_in,
    mask_in,
    vel_in,
    sig_in,
    cot_in,
    made,
    pack,
    corner_pack,
    local_sem,
    send_sem,
    recv_sem,
    self_sem,
    ready,
):
    lon = lax.axis_index("lon")
    lat = lax.axis_index("lat")
    top = lat == lat_count - 1
    inner = jnp.logical_not(top)
    has_south = lat > 0
    west = jnp.where(lon == 0, lon_count - 1, lon - 1)
    east = jnp.where(lon == lon_count - 1, 0, lon + 1)
    up = jnp.where(top, lat, lat + 1)
    down = jnp.where(has_south, lat - 1, lat)
    north_lon = jnp.where(top, lon_count - 1 - lon, lon)
    north_a = jnp.where(top, jnp.where(lon == 0, 0, lon_count - lon), west)
    north_b = jnp.where(top, lon_count - 2 - lon + jnp.where(lon == lon_count - 1, lon_count, 0), east)
    self_a = jnp.logical_and(top, north_a == lon)
    self_b = jnp.logical_and(top, north_b == lon)
    always = lat >= 0

    W, E, N, NA, NB, S, SA, SB = range(8)
    partner = [
        (west, lat),
        (east, lat),
        (north_lon, up),
        (north_a, up),
        (north_b, up),
        (lon, down),
        (west, down),
        (east, down),
    ]
    there = [always, always, always, jnp.logical_not(self_a), jnp.logical_not(self_b), has_south, has_south, has_south]
    reverse = [
        E,
        W,
        jnp.where(top, N, S),
        jnp.where(top, NA, SB),
        jnp.where(top, NB, SA),
        N,
        NB,
        NA,
    ]
    mine = start_order(lon, lat)
    plain = [(west, lat), (east, lat), (lon, up), (west, up), (east, up), (lon, down), (west, down), (east, down)]
    later = [start_order(*p) > mine for p in plain]
    folded = [jnp.logical_and(top, link in (N, NA, NB)) for link in range(8)]
    answers = [there[i] & jnp.logical_not(later[i]) & jnp.logical_not(folded[i]) for i in range(8)]
    awaits = [there[i] & later[i] & jnp.logical_not(folded[i]) for i in range(8)]
    greets = [there[i] & (later[i] | folded[i]) for i in range(8)]
    greeted = [there[i] & (jnp.logical_not(later[i]) | folded[i]) for i in range(8)]

    barrier = pltpu.get_barrier_semaphore()
    for link in range(8):

        @pl.when(greets[link])
        def _(link=link):
            pl.semaphore_signal(barrier, inc=1, device_id=partner[link], device_id_type=MESH)

    own = pl.ds(PAD, ROWS)
    loads = [
        pltpu.make_async_copy(wind, wind_in, local_sem.at[0]),
        pltpu.make_async_copy(mask, mask_in, local_sem.at[1]),
        pltpu.make_async_copy(vel, vel_in, local_sem.at[2]),
        pltpu.make_async_copy(sig, sig_in, local_sem.at[3]),
        pltpu.make_async_copy(strength, made.at[0], local_sem.at[4]),
        pltpu.make_async_copy(cot, cot_in, local_sem.at[5]),
    ]
    for copy in loads:
        copy.start()

    def send(src, dst, slot, sem, link):
        return pltpu.make_async_remote_copy(
            src_ref=src,
            dst_ref=dst,
            send_sem=send_sem.at[slot],
            recv_sem=recv_sem.at[sem],
            device_id=partner[link],
            device_id_type=MESH,
        )

    def rows_raw(row_of, to_of, slot, sem, link):
        return [
            send(arg.at[index + (pl.ds(row_of(n), n),)], ext.at[to + (pl.ds(to_of(n), n),)], slot + i, sem + i, link)
            for i, (arg, index, to, n) in enumerate(
                (
                    (vel, (slice(None),), (pl.ds(0, 2),), REACH),
                    (sig, (slice(None),), (pl.ds(2, 3),), REACH - 1),
                    (cot, (slice(None),), (pl.ds(NMAIN, 2),), BACK),
                )
            )
        ]

    def rows_made(row_of, to_of, slot, sem, link):
        n, m = REACH - 1, REACH - 2
        return [
            send(made.at[pl.ds(0, 2), pl.ds(row_of(n), n)], ext.at[pl.ds(5, 2), pl.ds(to_of(n), n)], slot + 3, sem + 3, link),
            send(made.at[pl.ds(2, 2), pl.ds(row_of(m), m)], ext.at[pl.ds(7, 2), pl.ds(to_of(m), m)], slot + 4, sem + 4, link),
        ]

    last = lambda n: ROWS - n
    to_low = lambda n: PAD - n
    to_fold = lambda n: EXT - n
    first = lambda n: 0
    to_high = lambda n: PAD + ROWS

    seven = (pl.ds(1, GROUP), pl.ds(0, GROUP))

    def corner(side, end, to, slot, sem, link):
        return send(corner_pack.at[side, end, :, seven[end]], corners.at[side, to, :, seven[end]], slot, sem, link)

    def self_corner(side):
        return pltpu.make_async_copy(
            corner_pack.at[side, 0, :, seven[0]], corners.at[side, 0, :, seven[0]], self_sem.at[side]
        )

    raw_low = rows_raw(last, to_low, 0, 5, N)
    raw_fold = rows_raw(last, to_fold, 0, 0, N)
    raw_high = rows_raw(first, to_high, 5, 0, S)
    made_low = rows_made(last, to_low, 0, 5, N)
    made_fold = rows_made(last, to_fold, 0, 0, N)
    made_high = rows_made(first, to_high, 5, 0, S)
    corners_low = [corner(i, 0, 1, 10 + i, 12 + i, NA + i) for i in range(2)]
    corners_fold = [corner(i, 0, 0, 10 + i, 10 + i, NA + i) for i in range(2)]
    corners_high = [corner(i, 1, 0, 12 + i, 10 + i, SA + i) for i in range(2)]
    strips_lon = [send(pack.at[0], land.at[0], 14, 14, W), send(pack.at[1], land.at[1], 15, 15, E)]

    def start_all(copies):
        for copy in copies:
            copy.start()

    def start_rows(link, part):
        def pick(raw, made_rows):
            return (raw[:1], raw[1:2], made_rows + raw[2:])[part]

        if link == N:
            pl.when(inner)(lambda: start_all(pick(raw_low, made_low)))
            pl.when(top)(lambda: start_all(pick(raw_fold, made_fold)))
        else:
            start_all(pick(raw_high, made_high))

    def start_strips(link):
        if link in (W, E):
            strips_lon[link - W].start()
        elif link in (NA, NB):
            pl.when(inner)(lambda: corners_low[link - NA].start())
            pl.when(top)(lambda: corners_fold[link - NA].start())
        else:
            corners_high[link - SA].start()

    count = sum(jnp.where(g, 1, 0) for g in greeted)
    pl.when(count > 0)(lambda: pl.semaphore_wait(barrier, count))
    for link in range(8):

        @pl.when(answers[link])
        def _(link=link):
            pl.semaphore_signal(ready.at[reverse[link]], inc=1, device_id=partner[link], device_id_type=MESH)

    for link in (N, S):
        pl.when(greeted[link])(lambda link=link: start_rows(link, 0))

    for copy in loads:
        copy.wait()
    made[1] = mask_in[...].astype(jnp.float32)
    made[2] = wind_in[0].astype(jnp.float32)
    made[3] = wind_in[1].astype(jnp.float32)
    block = [vel_in.at[0], vel_in.at[1], sig_in.at[0], sig_in.at[1], sig_in.at[2]]
    block += [made.at[0], made.at[1], made.at[2], made.at[3], cot_in.at[0], cot_in.at[1]]

    values = [ref[...] for ref in block]
    for side in range(2):
        for plane in range(2):
            at = [f for f in range(NFLD) if slot_of(f)[0] == plane]
            pack[side, plane] = strips([values[f] for f in at], [slot_of(f)[1:] for f in at], side, (ROWS, COLS))
        for end in range(2):
            for plane, slots in enumerate(corner_slots()):
                parts = [block[field][pl.ds(corner_rows(end, group), TILE)] for group, field, _, _ in slots]
                corner_pack[side, end, plane] = strips(parts, [slot[2:] for slot in slots], side, (TILE, COLS))

    for link in (NA, NB, SA, SB, W, E):
        pl.when(greeted[link])(lambda link=link: start_strips(link))
    patient = top & (lon < lon_count // 2)
    for part in (1, 2):
        for link in (N, S):
            wait = patient if link == N else jnp.logical_not(always)
            pl.when(greeted[link] & jnp.logical_not(wait))(lambda link=link, part=part: start_rows(link, part))

    for side, is_self in ((0, self_a), (1, self_b)):
        pl.when(is_self)(lambda side=side: self_corner(side).start())

    for link in (W, E, N, NA, NB, S, SA, SB):

        @pl.when(awaits[link])
        def _(link=link):
            pl.semaphore_wait(ready.at[link], 1)
            if link in (N, S):
                start_rows(link, 0)
                start_rows(link, 1)
                start_rows(link, 2)
            else:
                start_strips(link)

    for part in (1, 2):
        pl.when(patient)(lambda part=part: start_rows(N, part))

    def received(copies):
        for copy in copies:
            copy.wait_recv()

    def sent(copies):
        for copy in copies:
            copy.wait_send()

    received(strips_lon)
    received(raw_high + made_high)
    for side, is_self in ((0, self_a), (1, self_b)):

        pl.when(is_self)(lambda side=side: self_corner(side).wait())

        @pl.when(jnp.logical_not(is_self))
        def _(side=side):
            corners_high[side].wait_recv()
            corners_low[side].wait_send()

    @pl.when(has_south)
    def _():
        received(raw_low + made_low + corners_low)
        sent(raw_high + made_high + corners_high)

    sent(raw_low + made_low)
    sent(strips_lon)


def gather_halos(lon_count, lat_count, *operands):
    f32 = jnp.float32
    anywhere = pl.BlockSpec(memory_space=pl.ANY)
    return pl.pallas_call(
        partial(gather_kernel, lon_count, lat_count),
        out_shape=(
            jax.ShapeDtypeStruct((NFLD, EXT, COLS), f32),
            jax.ShapeDtypeStruct((2, 2, ROWS, COLS), f32),
            jax.ShapeDtypeStruct((2, 2, 3, TILE, COLS), f32),
        ),
        in_specs=[pl.BlockSpec(memory_space=pltpu.HBM)] * 6,
        out_specs=(anywhere, anywhere, anywhere),
        scratch_shapes=[
            pltpu.VMEM((2, ROWS, COLS), jnp.bfloat16),
            pltpu.VMEM((ROWS, COLS), jnp.int32),
            pltpu.VMEM((2, ROWS, COLS), f32),
            pltpu.VMEM((3, ROWS, COLS), f32),
            pltpu.VMEM((2, ROWS, COLS), f32),
            pltpu.VMEM((4, ROWS, COLS), f32),
            pltpu.VMEM((2, 2, ROWS, COLS), f32),
            pltpu.VMEM((2, 2, 3, TILE, COLS), f32),
            pltpu.SemaphoreType.DMA((6,)),
            pltpu.SemaphoreType.DMA((16,)),
            pltpu.SemaphoreType.DMA((16,)),
            pltpu.SemaphoreType.DMA((2,)),
            pltpu.SemaphoreType.REGULAR((8,)),
        ],
        compiler_params=pltpu.CompilerParams(
            collective_id=0, has_side_effects=True, vmem_limit_bytes=VMEM_LIMIT
        ),
    )(*operands)


def tiles_for(reach):
    low = (PAD - reach) // TILE
    high = -(-(PAD + ROWS + reach) // TILE)
    return range(low * TILE, high * TILE, TILE)


def working(raw):
    s1, s2, s12, strength, mask = raw
    cover = mask * (1.0 / 1.5)
    return [0.125 * (s1 + s2), 0.125 * (s1 - s2), 0.25 * s12, (1.0 / 16.0) * cover * strength, cover]


def flip_tile(value):
    value = jnp.take_along_axis(value, COLS - 1 - lane_ids(value.shape), axis=1)
    row = lax.broadcasted_iota(jnp.int32, value.shape, 0)
    return jnp.take_along_axis(value, TILE - 1 - row, axis=0)


def evp_kernel(
    lat_count,
    start,
    vel,
    sig,
    strength,
    wind,
    mask,
    cot,
    ext,
    land,
    corners,
    final_vel,
    vel_grad,
    sig_grad,
    fld,
    state,
    turn,
    saved,
    back,
    strain,
    carry,
):
    band = lax.axis_index("lat")
    top = band == lat_count - 1
    bottom = band == 0
    shape = (TILE, COLS)
    lane = lane_ids(shape)
    first_lane = lane == 0
    last_lane = lane == COLS - 1

    wind_f32 = wind[...].astype(jnp.float32)
    def store(plane, rows, q):
        q[2:7] = working(q[2:7])
        for field, value in enumerate(q):
            fld[field, plane, rows] = value

    for r in range(0, EXT, TILE):
        rows = pl.ds(r, TILE)
        if PAD <= r < PAD + ROWS:
            mine = pl.ds(r - PAD, TILE)
            at = slice(r - PAD, r - PAD + TILE)
            q = [vel[0, mine], vel[1, mine], sig[0, mine], sig[1, mine], sig[2, mine], strength[mine]]
            store(0, rows, q + [mask[mine].astype(jnp.float32), wind_f32[0, at], wind_f32[1, at], cot[0, mine], cot[1, mine]])
            q = []
            for field in range(NFLD):
                plane, to, width = slot_of(field)
                q.append(unstrip(land[0, plane, mine], land[1, plane, mine], to, width))
            store(1, rows, q)
        else:
            q = [ext[field, rows] for field in range(NFLD)]
            store(0, rows, [jnp.where(bottom, 0.0, x) for x in q] if r < PAD else q)

    def place_corners(end, turned):
        for group in range(3):
            q = [None] * NFLD
            for plane, slots in enumerate(corner_slots()):
                for of, field, to, width in slots:
                    if of == group:
                        q[field] = unstrip(corners[0, end, plane], corners[1, end, plane], to, width)
            q = [jnp.zeros(shape, jnp.float32) if x is None else x for x in q]
            if end == 1:
                q = [jnp.where(bottom, 0.0, x) for x in q]
            if turned:
                q = [-flip_tile(x) if field in ODD_FIELDS else flip_tile(x) for field, x in enumerate(q)]
            row = PAD + ROWS + GROUP * group if end == 0 else PAD - TILE - GROUP * group
            store(1, pl.ds(row, TILE), q)

    place_corners(1, False)
    pl.when(jnp.logical_not(top))(lambda: place_corners(0, False))
    pl.when(top)(lambda: place_corners(0, True))

    @pl.when(top)
    def _():
        for field in range(NFLD):
            old = [fld[field, 0, pl.ds(PAD + ROWS + t * TILE, TILE)] for t in range(3)]
            for t in range(3):
                new = flip_tile(old[2 - t])
                fld[field, 0, pl.ds(PAD + ROWS + t * TILE, TILE)] = -new if field in ODD_FIELDS else new

    for r in range(0, EXT, TILE):
        rows = pl.ds(r, TILE)
        row = band * ROWS + (r - PAD) + lax.broadcasted_iota(jnp.int32, shape, 0)
        total = ROWS * lat_count
        row = jnp.where(row >= total, 2 * total - 1 - row, row).astype(jnp.float32)
        half_f = 0.6 * ((2.0 * row + 1.0) / total - 1.0)
        scale = 1.5 / (2.25 + half_f * half_f)
        for plane in range(2):
            cover = fld[6, plane, rows]
            turn[0, plane, rows] = cover * (1.5 * scale)
            turn[1, plane, rows] = cover * (half_f * scale)

    def at(ref, lead, plane, r):
        if r < 0:
            return pltpu.roll(ref[lead + (plane, pl.ds(0, TILE))], 1, 0)
        if r > EXT - TILE:
            return pltpu.roll(ref[lead + (plane, pl.ds(EXT - TILE, TILE))], TILE - 1, 0)
        return ref[lead + (plane, pl.ds(r, TILE))]

    def lat_diff(ref, lead, r):
        return [at(ref, lead, p, r + 1) - at(ref, lead, p, r - 1) for p in range(2)]

    def lon_diff(ref, lead, r):
        here = [at(ref, lead, p, r) for p in range(2)]
        east = [pltpu.roll(x, COLS - 1, 1) for x in here]
        west = [pltpu.roll(x, 1, 1) for x in here]
        return [
            jnp.where(last_lane, east[1 - p], east[p]) - jnp.where(first_lane, west[1 - p], west[p])
            for p in range(2)
        ]

    start_value = start[0].astype(jnp.float32)
    for k in range(NSUB):
        src = fld if k == 0 else state
        left = NSUB - 1 - k
        keep = set(tiles_for(2 * k + 1))
        for r in tiles_for(11 + 2 * left):
            rows = pl.ds(r, TILE)
            dux = lon_diff(src, (0,), r)
            dvx = lon_diff(src, (1,), r)
            duy = lat_diff(src, (0,), r)
            dvy = lat_diff(src, (1,), r)
            for p in range(2):
                div = dux[p] + dvy[p]
                ten = dux[p] - dvy[p]
                she = duy[p] + dvx[p]
                inv = lax.rsqrt(div * div + 0.25 * (ten * ten + she * she) + 1.0)
                part = fld[5, p, rows]
                div = div * inv
                inv4 = 0.25 * inv
                ten = ten * inv4
                she = she * inv4
                if r in keep:
                    saved[k, 0, p, rows] = div
                    saved[k, 1, p, rows] = ten
                    saved[k, 2, p, rows] = she
                    saved[k, 3, p, rows] = part * inv
                cover = fld[6, p, rows]
                pull = div - 1.0
                state[2, p, rows] = cover * src[2, p, rows] + part * (pull + ten)
                state[3, p, rows] = cover * src[3, p, rows] + part * (pull - ten)
                state[4, p, rows] = cover * src[4, p, rows] + part * she
        weight = 0.5 * ((start_value + (k + 1)) / EVP_TOTAL)
        for r in tiles_for(0 if left == 0 else 10 + 2 * left):
            rows = pl.ds(r, TILE)
            dxx = lon_diff(state, (2,), r)
            dxy = lon_diff(state, (4,), r)
            dyx = lat_diff(state, (4,), r)
            dyy = lat_diff(state, (3,), r)
            for p in range(2):
                ru = src[0, p, rows] + (dxx[p] + dyx[p]) + weight * fld[7, p, rows]
                rv = src[1, p, rows] + (dxy[p] + dyy[p]) + weight * fld[8, p, rows]
                ca = turn[0, p, rows]
                cb = turn[1, p, rows]
                un = ca * ru + cb * rv
                vn = ca * rv - cb * ru
                if left == 0:
                    if p == 0:
                        final_vel[0, pl.ds(r - PAD, TILE)] = un
                        final_vel[1, pl.ds(r - PAD, TILE)] = vn
                else:
                    state[0, p, rows] = un
                    state[1, p, rows] = vn

    for r in tiles_for(BACK):
        rows = pl.ds(r, TILE)
        for p in range(2):
            gu = fld[9, p, rows]
            gv = fld[10, p, rows]
            ca = turn[0, p, rows]
            cb = turn[1, p, rows]
            back[0, p, rows] = ca * gu - cb * gv
            back[1, p, rows] = cb * gu + ca * gv

    for k in reversed(range(NSUB)):
        for r in tiles_for(2 * k + 1):
            rows = pl.ds(r, TILE)
            dux = lon_diff(back, (0,), r)
            dvx = lon_diff(back, (1,), r)
            duy = lat_diff(back, (0,), r)
            dvy = lat_diff(back, (1,), r)
            for p in range(2):
                gx = -dux[p]
                gy = -dvy[p]
                gz = -(duy[p] + dvx[p])
                if k < NSUB - 1:
                    gx = carry[0, p, rows] + gx
                    gy = carry[1, p, rows] + gy
                    gz = carry[2, p, rows] + gz
                both = gx + gy
                apart = gx - gy
                cover = fld[6, p, rows]
                if k > 0:
                    carry[0, p, rows] = cover * gx
                    carry[1, p, rows] = cover * gy
                    carry[2, p, rows] = cover * gz
                elif p == 0 and PAD <= r < PAD + ROWS:
                    out = pl.ds(r - PAD, TILE)
                    c8 = 0.125 * cover
                    sig_grad[0, out] = c8 * both
                    sig_grad[1, out] = c8 * apart
                    sig_grad[2, out] = (0.25 * cover) * gz
                div = saved[k, 0, p, rows]
                ten = saved[k, 1, p, rows]
                she = saved[k, 2, p, rows]
                part = saved[k, 3, p, rows]
                along = both * div + apart * ten + gz * she
                g_div = part * (both - along * div)
                g_ten = part * (0.25 * apart - along * ten)
                strain[0, p, rows] = g_div + g_ten
                strain[1, p, rows] = g_div - g_ten
                strain[2, p, rows] = part * (0.25 * gz - along * she)
        for r in tiles_for(2 * k):
            rows = pl.ds(r, TILE)
            dax = lon_diff(strain, (0,), r)
            dsx = lon_diff(strain, (2,), r)
            dsy = lat_diff(strain, (2,), r)
            dby = lat_diff(strain, (1,), r)
            for p in range(2):
                gu = back[0, p, rows] - (dax[p] + dsy[p])
                gv = back[1, p, rows] - (dsx[p] + dby[p])
                if k > 0:
                    ca = turn[0, p, rows]
                    cb = turn[1, p, rows]
                    back[0, p, rows] = ca * gu - cb * gv
                    back[1, p, rows] = cb * gu + ca * gv
                elif p == 0:
                    vel_grad[0, pl.ds(r - PAD, TILE)] = gu
                    vel_grad[1, pl.ds(r - PAD, TILE)] = gv


def evp_and_adjoint(lat_count, start, *operands):
    f32 = jnp.float32
    vmem = pl.BlockSpec(memory_space=pltpu.VMEM)
    return pl.pallas_call(
        partial(evp_kernel, lat_count),
        out_shape=(
            jax.ShapeDtypeStruct((2, ROWS, COLS), f32),
            jax.ShapeDtypeStruct((2, ROWS, COLS), f32),
            jax.ShapeDtypeStruct((3, ROWS, COLS), f32),
        ),
        in_specs=[pl.BlockSpec(memory_space=pltpu.SMEM)] + [vmem] * 9,
        out_specs=(vmem, vmem, vmem),
        scratch_shapes=[
            pltpu.VMEM((NFLD, 2, EXT, COLS), f32),
            pltpu.VMEM((5, 2, EXT, COLS), f32),
            pltpu.VMEM((2, 2, EXT, COLS), f32),
            pltpu.VMEM((NSUB, 4, 2, EXT, COLS), f32),
            pltpu.VMEM((2, 2, EXT, COLS), f32),
            pltpu.VMEM((3, 2, EXT, COLS), f32),
            pltpu.VMEM((3, 2, EXT, COLS), f32),
        ],
        compiler_params=pltpu.CompilerParams(vmem_limit_bytes=VMEM_LIMIT),
    )(start, *operands)


def shards(lon_count, lat_count, velocity, stress, strength, wind_stress, ice_mask, start_step, velocity_cotangent):
    block = (velocity, stress, strength, wind_stress, ice_mask, velocity_cotangent)
    halos = gather_halos(lon_count, lat_count, *(pltpu.with_memory_space_constraint(x, pltpu.HBM) for x in block))
    return evp_and_adjoint(lat_count, start_step, *block, *halos)


def solution(mesh):
    placed = (
        P(None, "lat", "lon"),
        P(None, "lat", "lon"),
        P("lat", "lon"),
        P(None, "lat", "lon"),
        P("lat", "lon"),
        P(),
        P(None, "lat", "lon"),
    )
    return jax.shard_map(
        partial(shards, mesh.shape["lon"], mesh.shape["lat"]),
        mesh=mesh,
        in_specs=placed,
        out_specs=(P(None, "lat", "lon"), P(None, "lat", "lon"), P(None, "lat", "lon")),
        check_vma=False,
    )
```

```python
from functools import partial

import jax
import jax.numpy as jnp
from jax import lax
from jax.experimental import pallas as pl
from jax.experimental.pallas import tpu as pltpu
from jax.sharding import PartitionSpec as P

NSUB = 6
EVP_TOTAL = 120
MESH = pl.DeviceIdType.MESH
VMEM_LIMIT = 32 * 1024 * 1024

ROWS = 48
COLS = 128
PAD = 24
EXT = ROWS + 2 * PAD
REACH = 22
BACK = 12
TILE = 8
NFLD = 11
NMAIN = 9
SLOT = 24

ODD_FIELDS = (0, 1, 7, 8, 9, 10)


GROUP = 7


def slot_of(field):
    if field < 5:
        return 0, SLOT * field, SLOT
    if field < NMAIN:
        return 1, SLOT * (field - 5), SLOT
    return 1, 4 * SLOT + BACK * (field - NMAIN), BACK


def corner_width(field, row):
    return (REACH, REACH, *(REACH - 1,) * 5, REACH - 2, REACH - 2, BACK, BACK)[field] - row


def corner_slots():
    wide = [(0, field, corner_width(field, 1)) for field in range(NFLD)]
    narrow = [(2, field, corner_width(field, 15)) for field in range(NMAIN)]
    planes = [wide[:6] + narrow[2:3], wide[6:] + narrow[:2] + narrow[3:]]
    planes.append([(1, field, corner_width(field, 8)) for field in range(NFLD)])
    placed = []
    for plane in planes:
        to = 0
        placed.append([])
        for group, field, width in plane:
            placed[-1].append((group, field, to, width))
            to += width
        assert to <= COLS
    return placed


def corner_rows(end, group):
    return ROWS - TILE - GROUP * group if end == 0 else GROUP * group


def strips(block, slots, side, shape):
    lanes = lane_ids(shape)
    packed = None
    for value, (to, width) in zip(block, slots):
        shift = (to - (0 if side == 0 else COLS - width)) % COLS
        if shift:
            value = pltpu.roll(value, shift, 1)
        packed = value if packed is None else jnp.where(lanes < to, packed, value)
    return packed


def unstrip(west, east, to, width):
    shift_a = (-to) % COLS
    shift_b = (COLS - width - to) % COLS
    if shift_a:
        west = pltpu.roll(west, shift_a, 1)
    if shift_b:
        east = pltpu.roll(east, shift_b, 1)
    return jnp.where(lane_ids(west.shape) < COLS // 2, west, east)


def lane_ids(shape):
    return lax.broadcasted_iota(jnp.int32, shape, len(shape) - 1)


def digit(value, size, count):
    return sum(jnp.where(value >= size * i, 1, 0) for i in range(1, count))


def start_order(lon, lat):
    y = digit(lon, 8, 4)
    z_low = digit(lon - 8 * y, 2, 4)
    x = digit(lat, 4, 4)
    z_high = lat - 4 * x
    early_half = z_high < 2
    base = jnp.where(early_half, 44 * z_high, jnp.where(z_high == 2, 130, 84))
    step = jnp.where(early_half, 13, 4)
    return 1024 * (7 * x + 7 * y + base + step * z_low) + 32 * lat + lon


def gather_kernel(
    lon_count,
    lat_count,
    vel,
    sig,
    strength,
    wind,
    mask,
    cot,
    ext,
    land,
    corners,
    wind_in,
    mask_in,
    vel_in,
    sig_in,
    cot_in,
    made,
    pack,
    corner_pack,
    local_sem,
    send_sem,
    recv_sem,
    self_sem,
    ready,
):
    lon = lax.axis_index("lon")
    lat = lax.axis_index("lat")
    top = lat == lat_count - 1
    inner = jnp.logical_not(top)
    has_south = lat > 0
    west = jnp.where(lon == 0, lon_count - 1, lon - 1)
    east = jnp.where(lon == lon_count - 1, 0, lon + 1)
    up = jnp.where(top, lat, lat + 1)
    down = jnp.where(has_south, lat - 1, lat)
    north_lon = jnp.where(top, lon_count - 1 - lon, lon)
    north_a = jnp.where(top, jnp.where(lon == 0, 0, lon_count - lon), west)
    north_b = jnp.where(top, lon_count - 2 - lon + jnp.where(lon == lon_count - 1, lon_count, 0), east)
    self_a = jnp.logical_and(top, north_a == lon)
    self_b = jnp.logical_and(top, north_b == lon)
    always = lat >= 0

    W, E, N, NA, NB, S, SA, SB = range(8)
    partner = [
        (west, lat),
        (east, lat),
        (north_lon, up),
        (north_a, up),
        (north_b, up),
        (lon, down),
        (west, down),
        (east, down),
    ]
    there = [always, always, always, jnp.logical_not(self_a), jnp.logical_not(self_b), has_south, has_south, has_south]
    reverse = [
        E,
        W,
        jnp.where(top, N, S),
        jnp.where(top, NA, SB),
        jnp.where(top, NB, SA),
        N,
        NB,
        NA,
    ]
    mine = start_order(lon, lat)
    plain = [(west, lat), (east, lat), (lon, up), (west, up), (east, up), (lon, down), (west, down), (east, down)]
    later = [start_order(*p) > mine for p in plain]
    folded = [jnp.logical_and(top, link in (N, NA, NB)) for link in range(8)]
    answers = [there[i] & jnp.logical_not(later[i]) & jnp.logical_not(folded[i]) for i in range(8)]
    awaits = [there[i] & later[i] & jnp.logical_not(folded[i]) for i in range(8)]
    greets = [there[i] & (later[i] | folded[i]) for i in range(8)]
    greeted = [there[i] & (jnp.logical_not(later[i]) | folded[i]) for i in range(8)]

    barrier = pltpu.get_barrier_semaphore()
    for link in range(8):

        @pl.when(greets[link])
        def _(link=link):
            pl.semaphore_signal(barrier, inc=1, device_id=partner[link], device_id_type=MESH)

    own = pl.ds(PAD, ROWS)
    loads = [
        pltpu.make_async_copy(wind, wind_in, local_sem.at[0]),
        pltpu.make_async_copy(mask, mask_in, local_sem.at[1]),
        pltpu.make_async_copy(vel, vel_in, local_sem.at[2]),
        pltpu.make_async_copy(sig, sig_in, local_sem.at[3]),
        pltpu.make_async_copy(strength, made.at[0], local_sem.at[4]),
        pltpu.make_async_copy(cot, cot_in, local_sem.at[5]),
    ]
    for copy in loads:
        copy.start()

    def send(src, dst, slot, sem, link):
        return pltpu.make_async_remote_copy(
            src_ref=src,
            dst_ref=dst,
            send_sem=send_sem.at[slot],
            recv_sem=recv_sem.at[sem],
            device_id=partner[link],
            device_id_type=MESH,
        )

    def rows_raw(row_of, to_of, slot, sem, link):
        return [
            send(arg.at[index + (pl.ds(row_of(n), n),)], ext.at[to + (pl.ds(to_of(n), n),)], slot + i, sem + i, link)
            for i, (arg, index, to, n) in enumerate(
                (
                    (vel, (slice(None),), (pl.ds(0, 2),), REACH),
                    (sig, (slice(None),), (pl.ds(2, 3),), REACH - 1),
                    (cot, (slice(None),), (pl.ds(NMAIN, 2),), BACK),
                )
            )
        ]

    def rows_made(row_of, to_of, slot, sem, link):
        n, m = REACH - 1, REACH - 2
        return [
            send(made.at[pl.ds(0, 2), pl.ds(row_of(n), n)], ext.at[pl.ds(5, 2), pl.ds(to_of(n), n)], slot + 3, sem + 3, link),
            send(made.at[pl.ds(2, 2), pl.ds(row_of(m), m)], ext.at[pl.ds(7, 2), pl.ds(to_of(m), m)], slot + 4, sem + 4, link),
        ]

    last = lambda n: ROWS - n
    to_low = lambda n: PAD - n
    to_fold = lambda n: EXT - n
    first = lambda n: 0
    to_high = lambda n: PAD + ROWS

    seven = (pl.ds(1, GROUP), pl.ds(0, GROUP))

    def corner(side, end, to, slot, sem, link):
        return send(corner_pack.at[side, end, :, seven[end]], corners.at[side, to, :, seven[end]], slot, sem, link)

    def self_corner(side):
        return pltpu.make_async_copy(
            corner_pack.at[side, 0, :, seven[0]], corners.at[side, 0, :, seven[0]], self_sem.at[side]
        )

    raw_low = rows_raw(last, to_low, 0, 5, N)
    raw_fold = rows_raw(last, to_fold, 0, 0, N)
    raw_high = rows_raw(first, to_high, 5, 0, S)
    made_low = rows_made(last, to_low, 0, 5, N)
    made_fold = rows_made(last, to_fold, 0, 0, N)
    made_high = rows_made(first, to_high, 5, 0, S)
    corners_low = [corner(i, 0, 1, 10 + i, 12 + i, NA + i) for i in range(2)]
    corners_fold = [corner(i, 0, 0, 10 + i, 10 + i, NA + i) for i in range(2)]
    corners_high = [corner(i, 1, 0, 12 + i, 10 + i, SA + i) for i in range(2)]
    strips_lon = [send(pack.at[0], land.at[0], 14, 14, W), send(pack.at[1], land.at[1], 15, 15, E)]

    def start_all(copies):
        for copy in copies:
            copy.start()

    def start_rows(link, part):
        def pick(raw, made_rows):
            return (raw[:1], raw[1:2], made_rows + raw[2:])[part]

        if link == N:
            pl.when(inner)(lambda: start_all(pick(raw_low, made_low)))
            pl.when(top)(lambda: start_all(pick(raw_fold, made_fold)))
        else:
            start_all(pick(raw_high, made_high))

    def start_strips(link):
        if link in (W, E):
            strips_lon[link - W].start()
        elif link in (NA, NB):
            pl.when(inner)(lambda: corners_low[link - NA].start())
            pl.when(top)(lambda: corners_fold[link - NA].start())
        else:
            corners_high[link - SA].start()

    count = sum(jnp.where(g, 1, 0) for g in greeted)
    pl.when(count > 0)(lambda: pl.semaphore_wait(barrier, count))
    patient = top & (lon < lon_count // 2)
    corners_first = inner & (lon == lon_count - 1)
    for link in (N, S):
        wait = corners_first | patient if link == N else corners_first
        pl.when(greeted[link] & jnp.logical_not(corners_first))(lambda link=link: start_rows(link, 0))
        pl.when(greeted[link] & jnp.logical_not(wait))(lambda link=link: start_rows(link, 1))

    for link in range(8):

        @pl.when(answers[link])
        def _(link=link):
            pl.semaphore_signal(ready.at[reverse[link]], inc=1, device_id=partner[link], device_id_type=MESH)


    for copy in loads:
        copy.wait()
    made[1] = mask_in[...].astype(jnp.float32)
    made[2] = wind_in[0].astype(jnp.float32)
    made[3] = wind_in[1].astype(jnp.float32)
    block = [vel_in.at[0], vel_in.at[1], sig_in.at[0], sig_in.at[1], sig_in.at[2]]
    block += [made.at[0], made.at[1], made.at[2], made.at[3], cot_in.at[0], cot_in.at[1]]

    values = [ref[...] for ref in block]
    for side in range(2):
        for plane in range(2):
            at = [f for f in range(NFLD) if slot_of(f)[0] == plane]
            pack[side, plane] = strips([values[f] for f in at], [slot_of(f)[1:] for f in at], side, (ROWS, COLS))
        for end in range(2):
            for plane, slots in enumerate(corner_slots()):
                parts = [block[field][pl.ds(corner_rows(end, group), TILE)] for group, field, _, _ in slots]
                corner_pack[side, end, plane] = strips(parts, [slot[2:] for slot in slots], side, (TILE, COLS))

    for link in (NB, SB, NA, SA, W, E):
        pl.when(greeted[link])(lambda link=link: start_strips(link))
    for link in (N, S):
        for part in (0, 1):
            pl.when(greeted[link] & corners_first)(lambda link=link, part=part: start_rows(link, part))
        wait = patient if link == N else jnp.logical_not(always)
        pl.when(greeted[link] & jnp.logical_not(wait))(lambda link=link: start_rows(link, 2))

    for side, is_self in ((0, self_a), (1, self_b)):
        pl.when(is_self)(lambda side=side: self_corner(side).start())

    for link in (W, E, N, S, NB, SB, NA, SA):

        @pl.when(awaits[link])
        def _(link=link):
            pl.semaphore_wait(ready.at[link], 1)
            if link in (N, S):
                start_rows(link, 0)
                start_rows(link, 1)
                start_rows(link, 2)
            else:
                start_strips(link)

    for part in (1, 2):
        pl.when(patient)(lambda part=part: start_rows(N, part))

    def received(copies):
        for copy in copies:
            copy.wait_recv()

    def sent(copies):
        for copy in copies:
            copy.wait_send()

    received(strips_lon)
    received(raw_high + made_high)
    for side, is_self in ((0, self_a), (1, self_b)):

        pl.when(is_self)(lambda side=side: self_corner(side).wait())

        @pl.when(jnp.logical_not(is_self))
        def _(side=side):
            corners_high[side].wait_recv()
            corners_low[side].wait_send()

    @pl.when(has_south)
    def _():
        received(raw_low + made_low + corners_low)
        sent(raw_high + made_high + corners_high)

    sent(raw_low + made_low)
    sent(strips_lon)


def gather_halos(lon_count, lat_count, *operands):
    f32 = jnp.float32
    anywhere = pl.BlockSpec(memory_space=pl.ANY)
    return pl.pallas_call(
        partial(gather_kernel, lon_count, lat_count),
        out_shape=(
            jax.ShapeDtypeStruct((NFLD, EXT, COLS), f32),
            jax.ShapeDtypeStruct((2, 2, ROWS, COLS), f32),
            jax.ShapeDtypeStruct((2, 2, 3, TILE, COLS), f32),
        ),
        in_specs=[pl.BlockSpec(memory_space=pltpu.HBM)] * 6,
        out_specs=(anywhere, anywhere, anywhere),
        scratch_shapes=[
            pltpu.VMEM((2, ROWS, COLS), jnp.bfloat16),
            pltpu.VMEM((ROWS, COLS), jnp.int32),
            pltpu.VMEM((2, ROWS, COLS), f32),
            pltpu.VMEM((3, ROWS, COLS), f32),
            pltpu.VMEM((2, ROWS, COLS), f32),
            pltpu.VMEM((4, ROWS, COLS), f32),
            pltpu.VMEM((2, 2, ROWS, COLS), f32),
            pltpu.VMEM((2, 2, 3, TILE, COLS), f32),
            pltpu.SemaphoreType.DMA((6,)),
            pltpu.SemaphoreType.DMA((16,)),
            pltpu.SemaphoreType.DMA((16,)),
            pltpu.SemaphoreType.DMA((2,)),
            pltpu.SemaphoreType.REGULAR((8,)),
        ],
        compiler_params=pltpu.CompilerParams(
            collective_id=0, has_side_effects=True, vmem_limit_bytes=VMEM_LIMIT
        ),
    )(*operands)


def tiles_for(reach):
    low = (PAD - reach) // TILE
    high = -(-(PAD + ROWS + reach) // TILE)
    return range(low * TILE, high * TILE, TILE)


def working(raw):
    s1, s2, s12, strength, mask = raw
    cover = mask * (1.0 / 1.5)
    return [0.125 * (s1 + s2), 0.125 * (s1 - s2), 0.25 * s12, (1.0 / 16.0) * cover * strength, cover]


def flip_tile(value):
    value = jnp.take_along_axis(value, COLS - 1 - lane_ids(value.shape), axis=1)
    row = lax.broadcasted_iota(jnp.int32, value.shape, 0)
    return jnp.take_along_axis(value, TILE - 1 - row, axis=0)


def evp_kernel(
    lat_count,
    start,
    vel,
    sig,
    strength,
    wind,
    mask,
    cot,
    ext,
    land,
    corners,
    final_vel,
    vel_grad,
    sig_grad,
    fld,
    state,
    turn,
    saved,
    back,
    strain,
    carry,
):
    band = lax.axis_index("lat")
    top = band == lat_count - 1
    bottom = band == 0
    shape = (TILE, COLS)
    lane = lane_ids(shape)
    first_lane = lane == 0
    last_lane = lane == COLS - 1

    wind_f32 = wind[...].astype(jnp.float32)
    def store(plane, rows, q):
        q[2:7] = working(q[2:7])
        for field, value in enumerate(q):
            fld[field, plane, rows] = value

    for r in range(0, EXT, TILE):
        rows = pl.ds(r, TILE)
        if PAD <= r < PAD + ROWS:
            mine = pl.ds(r - PAD, TILE)
            at = slice(r - PAD, r - PAD + TILE)
            q = [vel[0, mine], vel[1, mine], sig[0, mine], sig[1, mine], sig[2, mine], strength[mine]]
            store(0, rows, q + [mask[mine].astype(jnp.float32), wind_f32[0, at], wind_f32[1, at], cot[0, mine], cot[1, mine]])
            q = []
            for field in range(NFLD):
                plane, to, width = slot_of(field)
                q.append(unstrip(land[0, plane, mine], land[1, plane, mine], to, width))
            store(1, rows, q)
        else:
            q = [ext[field, rows] for field in range(NFLD)]
            store(0, rows, [jnp.where(bottom, 0.0, x) for x in q] if r < PAD else q)

    def place_corners(end, turned):
        for group in range(3):
            q = [None] * NFLD
            for plane, slots in enumerate(corner_slots()):
                for of, field, to, width in slots:
                    if of == group:
                        q[field] = unstrip(corners[0, end, plane], corners[1, end, plane], to, width)
            q = [jnp.zeros(shape, jnp.float32) if x is None else x for x in q]
            if end == 1:
                q = [jnp.where(bottom, 0.0, x) for x in q]
            if turned:
                q = [-flip_tile(x) if field in ODD_FIELDS else flip_tile(x) for field, x in enumerate(q)]
            row = PAD + ROWS + GROUP * group if end == 0 else PAD - TILE - GROUP * group
            store(1, pl.ds(row, TILE), q)

    place_corners(1, False)
    pl.when(jnp.logical_not(top))(lambda: place_corners(0, False))
    pl.when(top)(lambda: place_corners(0, True))

    @pl.when(top)
    def _():
        for field in range(NFLD):
            old = [fld[field, 0, pl.ds(PAD + ROWS + t * TILE, TILE)] for t in range(3)]
            for t in range(3):
                new = flip_tile(old[2 - t])
                fld[field, 0, pl.ds(PAD + ROWS + t * TILE, TILE)] = -new if field in ODD_FIELDS else new

    for r in range(0, EXT, TILE):
        rows = pl.ds(r, TILE)
        row = band * ROWS + (r - PAD) + lax.broadcasted_iota(jnp.int32, shape, 0)
        total = ROWS * lat_count
        row = jnp.where(row >= total, 2 * total - 1 - row, row).astype(jnp.float32)
        half_f = 0.6 * ((2.0 * row + 1.0) / total - 1.0)
        scale = 1.5 / (2.25 + half_f * half_f)
        for plane in range(2):
            cover = fld[6, plane, rows]
            turn[0, plane, rows] = cover * (1.5 * scale)
            turn[1, plane, rows] = cover * (half_f * scale)

    def at(ref, lead, plane, r):
        if r < 0:
            return pltpu.roll(ref[lead + (plane, pl.ds(0, TILE))], 1, 0)
        if r > EXT - TILE:
            return pltpu.roll(ref[lead + (plane, pl.ds(EXT - TILE, TILE))], TILE - 1, 0)
        return ref[lead + (plane, pl.ds(r, TILE))]

    def lat_diff(ref, lead, r):
        return [at(ref, lead, p, r + 1) - at(ref, lead, p, r - 1) for p in range(2)]

    def lon_diff(ref, lead, r):
        here = [at(ref, lead, p, r) for p in range(2)]
        east = [pltpu.roll(x, COLS - 1, 1) for x in here]
        west = [pltpu.roll(x, 1, 1) for x in here]
        return [
            jnp.where(last_lane, east[1 - p], east[p]) - jnp.where(first_lane, west[1 - p], west[p])
            for p in range(2)
        ]

    start_value = start[0].astype(jnp.float32)
    for k in range(NSUB):
        src = fld if k == 0 else state
        left = NSUB - 1 - k
        keep = set(tiles_for(2 * k + 1))
        for r in tiles_for(11 + 2 * left):
            rows = pl.ds(r, TILE)
            dux = lon_diff(src, (0,), r)
            dvx = lon_diff(src, (1,), r)
            duy = lat_diff(src, (0,), r)
            dvy = lat_diff(src, (1,), r)
            for p in range(2):
                div = dux[p] + dvy[p]
                ten = dux[p] - dvy[p]
                she = duy[p] + dvx[p]
                inv = lax.rsqrt(div * div + 0.25 * (ten * ten + she * she) + 1.0)
                part = fld[5, p, rows]
                div = div * inv
                inv4 = 0.25 * inv
                ten = ten * inv4
                she = she * inv4
                if r in keep:
                    saved[k, 0, p, rows] = div
                    saved[k, 1, p, rows] = ten
                    saved[k, 2, p, rows] = she
                    saved[k, 3, p, rows] = part * inv
                cover = fld[6, p, rows]
                pull = div - 1.0
                state[2, p, rows] = cover * src[2, p, rows] + part * (pull + ten)
                state[3, p, rows] = cover * src[3, p, rows] + part * (pull - ten)
                state[4, p, rows] = cover * src[4, p, rows] + part * she
        weight = 0.5 * ((start_value + (k + 1)) / EVP_TOTAL)
        for r in tiles_for(0 if left == 0 else 10 + 2 * left):
            rows = pl.ds(r, TILE)
            dxx = lon_diff(state, (2,), r)
            dxy = lon_diff(state, (4,), r)
            dyx = lat_diff(state, (4,), r)
            dyy = lat_diff(state, (3,), r)
            for p in range(2):
                ru = src[0, p, rows] + (dxx[p] + dyx[p]) + weight * fld[7, p, rows]
                rv = src[1, p, rows] + (dxy[p] + dyy[p]) + weight * fld[8, p, rows]
                ca = turn[0, p, rows]
                cb = turn[1, p, rows]
                un = ca * ru + cb * rv
                vn = ca * rv - cb * ru
                if left == 0:
                    if p == 0:
                        final_vel[0, pl.ds(r - PAD, TILE)] = un
                        final_vel[1, pl.ds(r - PAD, TILE)] = vn
                else:
                    state[0, p, rows] = un
                    state[1, p, rows] = vn

    for r in tiles_for(BACK):
        rows = pl.ds(r, TILE)
        for p in range(2):
            gu = fld[9, p, rows]
            gv = fld[10, p, rows]
            ca = turn[0, p, rows]
            cb = turn[1, p, rows]
            back[0, p, rows] = ca * gu - cb * gv
            back[1, p, rows] = cb * gu + ca * gv

    for k in reversed(range(NSUB)):
        for r in tiles_for(2 * k + 1):
            rows = pl.ds(r, TILE)
            dux = lon_diff(back, (0,), r)
            dvx = lon_diff(back, (1,), r)
            duy = lat_diff(back, (0,), r)
            dvy = lat_diff(back, (1,), r)
            for p in range(2):
                gx = -dux[p]
                gy = -dvy[p]
                gz = -(duy[p] + dvx[p])
                if k < NSUB - 1:
                    gx = carry[0, p, rows] + gx
                    gy = carry[1, p, rows] + gy
                    gz = carry[2, p, rows] + gz
                both = gx + gy
                apart = gx - gy
                cover = fld[6, p, rows]
                if k > 0:
                    carry[0, p, rows] = cover * gx
                    carry[1, p, rows] = cover * gy
                    carry[2, p, rows] = cover * gz
                elif p == 0 and PAD <= r < PAD + ROWS:
                    out = pl.ds(r - PAD, TILE)
                    c8 = 0.125 * cover
                    sig_grad[0, out] = c8 * both
                    sig_grad[1, out] = c8 * apart
                    sig_grad[2, out] = (0.25 * cover) * gz
                div = saved[k, 0, p, rows]
                ten = saved[k, 1, p, rows]
                she = saved[k, 2, p, rows]
                part = saved[k, 3, p, rows]
                along = both * div + apart * ten + gz * she
                g_div = part * (both - along * div)
                g_ten = part * (0.25 * apart - along * ten)
                strain[0, p, rows] = g_div + g_ten
                strain[1, p, rows] = g_div - g_ten
                strain[2, p, rows] = part * (0.25 * gz - along * she)
        for r in tiles_for(2 * k):
            rows = pl.ds(r, TILE)
            dax = lon_diff(strain, (0,), r)
            dsx = lon_diff(strain, (2,), r)
            dsy = lat_diff(strain, (2,), r)
            dby = lat_diff(strain, (1,), r)
            for p in range(2):
                gu = back[0, p, rows] - (dax[p] + dsy[p])
                gv = back[1, p, rows] - (dsx[p] + dby[p])
                if k > 0:
                    ca = turn[0, p, rows]
                    cb = turn[1, p, rows]
                    back[0, p, rows] = ca * gu - cb * gv
                    back[1, p, rows] = cb * gu + ca * gv
                elif p == 0:
                    vel_grad[0, pl.ds(r - PAD, TILE)] = gu
                    vel_grad[1, pl.ds(r - PAD, TILE)] = gv


def evp_and_adjoint(lat_count, start, *operands):
    f32 = jnp.float32
    vmem = pl.BlockSpec(memory_space=pltpu.VMEM)
    return pl.pallas_call(
        partial(evp_kernel, lat_count),
        out_shape=(
            jax.ShapeDtypeStruct((2, ROWS, COLS), f32),
            jax.ShapeDtypeStruct((2, ROWS, COLS), f32),
            jax.ShapeDtypeStruct((3, ROWS, COLS), f32),
        ),
        in_specs=[pl.BlockSpec(memory_space=pltpu.SMEM)] + [vmem] * 9,
        out_specs=(vmem, vmem, vmem),
        scratch_shapes=[
            pltpu.VMEM((NFLD, 2, EXT, COLS), f32),
            pltpu.VMEM((5, 2, EXT, COLS), f32),
            pltpu.VMEM((2, 2, EXT, COLS), f32),
            pltpu.VMEM((NSUB, 4, 2, EXT, COLS), f32),
            pltpu.VMEM((2, 2, EXT, COLS), f32),
            pltpu.VMEM((3, 2, EXT, COLS), f32),
            pltpu.VMEM((3, 2, EXT, COLS), f32),
        ],
        compiler_params=pltpu.CompilerParams(vmem_limit_bytes=VMEM_LIMIT),
    )(start, *operands)


def shards(lon_count, lat_count, velocity, stress, strength, wind_stress, ice_mask, start_step, velocity_cotangent):
    block = (velocity, stress, strength, wind_stress, ice_mask, velocity_cotangent)
    halos = gather_halos(lon_count, lat_count, *(pltpu.with_memory_space_constraint(x, pltpu.HBM) for x in block))
    return evp_and_adjoint(lat_count, start_step, *block, *halos)


def solution(mesh):
    placed = (
        P(None, "lat", "lon"),
        P(None, "lat", "lon"),
        P("lat", "lon"),
        P(None, "lat", "lon"),
        P("lat", "lon"),
        P(),
        P(None, "lat", "lon"),
    )
    return jax.shard_map(
        partial(shards, mesh.shape["lon"], mesh.shape["lat"]),
        mesh=mesh,
        in_specs=placed,
        out_specs=(P(None, "lat", "lon"), P(None, "lat", "lon"), P(None, "lat", "lon")),
        check_vma=False,
    )
```

```python
from functools import partial

import jax
import jax.numpy as jnp
from jax import lax
from jax.experimental import pallas as pl
from jax.experimental.pallas import tpu as pltpu
from jax.sharding import PartitionSpec as P

NSUB = 6
EVP_TOTAL = 120
MESH = pl.DeviceIdType.MESH
VMEM_LIMIT = 32 * 1024 * 1024

ROWS = 48
COLS = 128
PAD = 24
EXT = ROWS + 2 * PAD
REACH = 22
BACK = 12
TILE = 8
NFLD = 11
NMAIN = 9
SLOT = 24

ODD_FIELDS = (0, 1, 7, 8, 9, 10)


GROUP = 7


def slot_of(field):
    if field < 5:
        return 0, SLOT * field, SLOT
    if field < NMAIN:
        return 1, SLOT * (field - 5), SLOT
    return 1, 4 * SLOT + BACK * (field - NMAIN), BACK


def corner_width(field, row):
    return (REACH, REACH, *(REACH - 1,) * 5, REACH - 2, REACH - 2, BACK, BACK)[field] - row


def corner_slots():
    wide = [(0, field, corner_width(field, 1)) for field in range(NFLD)]
    narrow = [(2, field, corner_width(field, 15)) for field in range(NMAIN)]
    planes = [wide[:6] + narrow[2:3], wide[6:] + narrow[:2] + narrow[3:]]
    planes.append([(1, field, corner_width(field, 8)) for field in range(NFLD)])
    placed = []
    for plane in planes:
        to = 0
        placed.append([])
        for group, field, width in plane:
            placed[-1].append((group, field, to, width))
            to += width
        assert to <= COLS
    return placed


def corner_rows(end, group):
    return ROWS - TILE - GROUP * group if end == 0 else GROUP * group


def strips(block, slots, side, shape):
    lanes = lane_ids(shape)
    packed = None
    for value, (to, width) in zip(block, slots):
        shift = (to - (0 if side == 0 else COLS - width)) % COLS
        if shift:
            value = pltpu.roll(value, shift, 1)
        packed = value if packed is None else jnp.where(lanes < to, packed, value)
    return packed


def unstrip(west, east, to, width):
    shift_a = (-to) % COLS
    shift_b = (COLS - width - to) % COLS
    if shift_a:
        west = pltpu.roll(west, shift_a, 1)
    if shift_b:
        east = pltpu.roll(east, shift_b, 1)
    return jnp.where(lane_ids(west.shape) < COLS // 2, west, east)


def lane_ids(shape):
    return lax.broadcasted_iota(jnp.int32, shape, len(shape) - 1)


def digit(value, size, count):
    return sum(jnp.where(value >= size * i, 1, 0) for i in range(1, count))


def start_order(lon, lat):
    y = digit(lon, 8, 4)
    z_low = digit(lon - 8 * y, 2, 4)
    x = digit(lat, 4, 4)
    z_high = lat - 4 * x
    early_half = z_high < 2
    base = jnp.where(early_half, 44 * z_high, jnp.where(z_high == 2, 130, 84))
    step = jnp.where(early_half, 13, 4)
    return 1024 * (7 * x + 7 * y + base + step * z_low) + 32 * lat + lon


def gather_kernel(
    lon_count,
    lat_count,
    vel,
    sig,
    strength,
    wind,
    mask,
    cot,
    ext,
    land,
    corners,
    wind_in,
    mask_in,
    vel_in,
    sig_in,
    cot_in,
    made,
    pack,
    corner_pack,
    local_sem,
    send_sem,
    recv_sem,
    self_sem,
    ready,
):
    lon = lax.axis_index("lon")
    lat = lax.axis_index("lat")
    top = lat == lat_count - 1
    inner = jnp.logical_not(top)
    has_south = lat > 0
    west = jnp.where(lon == 0, lon_count - 1, lon - 1)
    east = jnp.where(lon == lon_count - 1, 0, lon + 1)
    up = jnp.where(top, lat, lat + 1)
    down = jnp.where(has_south, lat - 1, lat)
    north_lon = jnp.where(top, lon_count - 1 - lon, lon)
    north_a = jnp.where(top, jnp.where(lon == 0, 0, lon_count - lon), west)
    north_b = jnp.where(top, lon_count - 2 - lon + jnp.where(lon == lon_count - 1, lon_count, 0), east)
    self_a = jnp.logical_and(top, north_a == lon)
    self_b = jnp.logical_and(top, north_b == lon)
    always = lat >= 0

    W, E, N, NA, NB, S, SA, SB = range(8)
    partner = [
        (west, lat),
        (east, lat),
        (north_lon, up),
        (north_a, up),
        (north_b, up),
        (lon, down),
        (west, down),
        (east, down),
    ]
    there = [always, always, always, jnp.logical_not(self_a), jnp.logical_not(self_b), has_south, has_south, has_south]
    reverse = [
        E,
        W,
        jnp.where(top, N, S),
        jnp.where(top, NA, SB),
        jnp.where(top, NB, SA),
        N,
        NB,
        NA,
    ]
    mine = start_order(lon, lat)
    plain = [(west, lat), (east, lat), (lon, up), (west, up), (east, up), (lon, down), (west, down), (east, down)]
    later = [start_order(*p) > mine for p in plain]
    folded = [jnp.logical_and(top, link in (N, NA, NB)) for link in range(8)]
    answers = [there[i] & jnp.logical_not(later[i]) & jnp.logical_not(folded[i]) for i in range(8)]
    awaits = [there[i] & later[i] & jnp.logical_not(folded[i]) for i in range(8)]
    greets = [there[i] & (later[i] | folded[i]) for i in range(8)]
    greeted = [there[i] & (jnp.logical_not(later[i]) | folded[i]) for i in range(8)]

    barrier = pltpu.get_barrier_semaphore()
    for link in range(8):

        @pl.when(greets[link])
        def _(link=link):
            pl.semaphore_signal(barrier, inc=1, device_id=partner[link], device_id_type=MESH)

    own = pl.ds(PAD, ROWS)
    loads = [
        pltpu.make_async_copy(wind, wind_in, local_sem.at[0]),
        pltpu.make_async_copy(mask, mask_in, local_sem.at[1]),
        pltpu.make_async_copy(vel, vel_in, local_sem.at[2]),
        pltpu.make_async_copy(sig, sig_in, local_sem.at[3]),
        pltpu.make_async_copy(strength, made.at[0], local_sem.at[4]),
        pltpu.make_async_copy(cot, cot_in, local_sem.at[5]),
    ]
    for copy in loads:
        copy.start()

    def send(src, dst, slot, sem, link):
        return pltpu.make_async_remote_copy(
            src_ref=src,
            dst_ref=dst,
            send_sem=send_sem.at[slot],
            recv_sem=recv_sem.at[sem],
            device_id=partner[link],
            device_id_type=MESH,
        )

    def rows_raw(row_of, to_of, slot, sem, link):
        return [
            send(arg.at[index + (pl.ds(row_of(n), n),)], ext.at[to + (pl.ds(to_of(n), n),)], slot + i, sem + i, link)
            for i, (arg, index, to, n) in enumerate(
                (
                    (vel, (slice(None),), (pl.ds(0, 2),), REACH),
                    (sig, (slice(None),), (pl.ds(2, 3),), REACH - 1),
                    (cot, (slice(None),), (pl.ds(NMAIN, 2),), BACK),
                )
            )
        ]

    def rows_made(row_of, to_of, slot, sem, link):
        n, m = REACH - 1, REACH - 2
        return [
            send(made.at[pl.ds(0, 2), pl.ds(row_of(n), n)], ext.at[pl.ds(5, 2), pl.ds(to_of(n), n)], slot + 3, sem + 3, link),
            send(made.at[pl.ds(2, 2), pl.ds(row_of(m), m)], ext.at[pl.ds(7, 2), pl.ds(to_of(m), m)], slot + 4, sem + 4, link),
        ]

    last = lambda n: ROWS - n
    to_low = lambda n: PAD - n
    to_fold = lambda n: EXT - n
    first = lambda n: 0
    to_high = lambda n: PAD + ROWS

    seven = (pl.ds(1, GROUP), pl.ds(0, GROUP))

    def corner(side, end, to, slot, sem, link):
        return send(corner_pack.at[side, end, :, seven[end]], corners.at[side, to, :, seven[end]], slot, sem, link)

    def self_corner(side):
        return pltpu.make_async_copy(
            corner_pack.at[side, 0, :, seven[0]], corners.at[side, 0, :, seven[0]], self_sem.at[side]
        )

    raw_low = rows_raw(last, to_low, 0, 5, N)
    raw_fold = rows_raw(last, to_fold, 0, 0, N)
    raw_high = rows_raw(first, to_high, 5, 0, S)
    made_low = rows_made(last, to_low, 0, 5, N)
    made_fold = rows_made(last, to_fold, 0, 0, N)
    made_high = rows_made(first, to_high, 5, 0, S)
    corners_low = [corner(i, 0, 1, 10 + i, 12 + i, NA + i) for i in range(2)]
    corners_fold = [corner(i, 0, 0, 10 + i, 10 + i, NA + i) for i in range(2)]
    corners_high = [corner(i, 1, 0, 12 + i, 10 + i, SA + i) for i in range(2)]
    strips_lon = [send(pack.at[0], land.at[0], 14, 14, W), send(pack.at[1], land.at[1], 15, 15, E)]

    def start_all(copies):
        for copy in copies:
            copy.start()

    def start_rows(link, part):
        def pick(raw, made_rows):
            return (raw[:1], raw[1:2], made_rows + raw[2:])[part]

        if link == N:
            pl.when(inner)(lambda: start_all(pick(raw_low, made_low)))
            pl.when(top)(lambda: start_all(pick(raw_fold, made_fold)))
        else:
            start_all(pick(raw_high, made_high))

    def start_strips(link):
        if link in (W, E):
            strips_lon[link - W].start()
        elif link in (NA, NB):
            pl.when(inner)(lambda: corners_low[link - NA].start())
            pl.when(top)(lambda: corners_fold[link - NA].start())
        else:
            corners_high[link - SA].start()

    count = sum(jnp.where(g, 1, 0) for g in greeted)
    pl.when(count > 0)(lambda: pl.semaphore_wait(barrier, count))
    for link in (N, S, NB, SB, NA, SA, W, E):

        @pl.when(answers[link])
        def _(link=link):
            pl.semaphore_signal(ready.at[reverse[link]], inc=1, device_id=partner[link], device_id_type=MESH)


    patient = top & (lon < lon_count // 2)
    corners_first = inner & (lon == lon_count - 1)
    for link in (N, S):
        wait = corners_first | patient if link == N else corners_first
        pl.when(greeted[link] & jnp.logical_not(corners_first))(lambda link=link: start_rows(link, 0))
        pl.when(greeted[link] & jnp.logical_not(wait))(lambda link=link: start_rows(link, 1))

    for copy in loads:
        copy.wait()
    made[1] = mask_in[...].astype(jnp.float32)
    made[2] = wind_in[0].astype(jnp.float32)
    made[3] = wind_in[1].astype(jnp.float32)
    block = [vel_in.at[0], vel_in.at[1], sig_in.at[0], sig_in.at[1], sig_in.at[2]]
    block += [made.at[0], made.at[1], made.at[2], made.at[3], cot_in.at[0], cot_in.at[1]]

    values = [ref[...] for ref in block]
    for side in range(2):
        for plane in range(2):
            at = [f for f in range(NFLD) if slot_of(f)[0] == plane]
            pack[side, plane] = strips([values[f] for f in at], [slot_of(f)[1:] for f in at], side, (ROWS, COLS))
        for end in range(2):
            for plane, slots in enumerate(corner_slots()):
                parts = [block[field][pl.ds(corner_rows(end, group), TILE)] for group, field, _, _ in slots]
                corner_pack[side, end, plane] = strips(parts, [slot[2:] for slot in slots], side, (TILE, COLS))

    for link in (NB, SB, NA, SA, W, E):
        pl.when(greeted[link])(lambda link=link: start_strips(link))
    for link in (N, S):
        for part in (0, 1):
            pl.when(greeted[link] & corners_first)(lambda link=link, part=part: start_rows(link, part))
        wait = patient if link == N else jnp.logical_not(always)
        pl.when(greeted[link] & jnp.logical_not(wait))(lambda link=link: start_rows(link, 2))

    for side, is_self in ((0, self_a), (1, self_b)):
        pl.when(is_self)(lambda side=side: self_corner(side).start())

    for link in (W, E, N, S, NB, SB, NA, SA):

        @pl.when(awaits[link])
        def _(link=link):
            pl.semaphore_wait(ready.at[link], 1)
            if link in (N, S):
                start_rows(link, 0)
                start_rows(link, 1)
                start_rows(link, 2)
            else:
                start_strips(link)

    for part in (1, 2):
        pl.when(patient)(lambda part=part: start_rows(N, part))

    def received(copies):
        for copy in copies:
            copy.wait_recv()

    def sent(copies):
        for copy in copies:
            copy.wait_send()

    received(strips_lon)
    received(raw_high + made_high)
    for side, is_self in ((0, self_a), (1, self_b)):

        pl.when(is_self)(lambda side=side: self_corner(side).wait())

        @pl.when(jnp.logical_not(is_self))
        def _(side=side):
            corners_high[side].wait_recv()
            corners_low[side].wait_send()

    @pl.when(has_south)
    def _():
        received(raw_low + made_low + corners_low)
        sent(raw_high + made_high + corners_high)

    sent(raw_low + made_low)
    sent(strips_lon)


def gather_halos(lon_count, lat_count, *operands):
    f32 = jnp.float32
    anywhere = pl.BlockSpec(memory_space=pl.ANY)
    return pl.pallas_call(
        partial(gather_kernel, lon_count, lat_count),
        out_shape=(
            jax.ShapeDtypeStruct((NFLD, EXT, COLS), f32),
            jax.ShapeDtypeStruct((2, 2, ROWS, COLS), f32),
            jax.ShapeDtypeStruct((2, 2, 3, TILE, COLS), f32),
        ),
        in_specs=[pl.BlockSpec(memory_space=pltpu.HBM)] * 6,
        out_specs=(anywhere, anywhere, anywhere),
        scratch_shapes=[
            pltpu.VMEM((2, ROWS, COLS), jnp.bfloat16),
            pltpu.VMEM((ROWS, COLS), jnp.int32),
            pltpu.VMEM((2, ROWS, COLS), f32),
            pltpu.VMEM((3, ROWS, COLS), f32),
            pltpu.VMEM((2, ROWS, COLS), f32),
            pltpu.VMEM((4, ROWS, COLS), f32),
            pltpu.VMEM((2, 2, ROWS, COLS), f32),
            pltpu.VMEM((2, 2, 3, TILE, COLS), f32),
            pltpu.SemaphoreType.DMA((6,)),
            pltpu.SemaphoreType.DMA((16,)),
            pltpu.SemaphoreType.DMA((16,)),
            pltpu.SemaphoreType.DMA((2,)),
            pltpu.SemaphoreType.REGULAR((8,)),
        ],
        compiler_params=pltpu.CompilerParams(
            collective_id=0, has_side_effects=True, vmem_limit_bytes=VMEM_LIMIT
        ),
    )(*operands)


def tiles_for(reach):
    low = (PAD - reach) // TILE
    high = -(-(PAD + ROWS + reach) // TILE)
    return range(low * TILE, high * TILE, TILE)


def working(raw):
    s1, s2, s12, strength, mask = raw
    cover = mask * (1.0 / 1.5)
    return [0.125 * (s1 + s2), 0.125 * (s1 - s2), 0.25 * s12, (1.0 / 16.0) * cover * strength, cover]


def flip_tile(value):
    value = jnp.take_along_axis(value, COLS - 1 - lane_ids(value.shape), axis=1)
    row = lax.broadcasted_iota(jnp.int32, value.shape, 0)
    return jnp.take_along_axis(value, TILE - 1 - row, axis=0)


def evp_kernel(
    lat_count,
    start,
    vel,
    sig,
    strength,
    wind,
    mask,
    cot,
    ext,
    land,
    corners,
    final_vel,
    vel_grad,
    sig_grad,
    fld,
    state,
    turn,
    saved,
    back,
    strain,
    carry,
):
    band = lax.axis_index("lat")
    top = band == lat_count - 1
    bottom = band == 0
    shape = (TILE, COLS)
    lane = lane_ids(shape)
    first_lane = lane == 0
    last_lane = lane == COLS - 1

    wind_f32 = wind[...].astype(jnp.float32)
    def store(plane, rows, q):
        q[2:7] = working(q[2:7])
        for field, value in enumerate(q):
            fld[field, plane, rows] = value

    for r in range(0, EXT, TILE):
        rows = pl.ds(r, TILE)
        if PAD <= r < PAD + ROWS:
            mine = pl.ds(r - PAD, TILE)
            at = slice(r - PAD, r - PAD + TILE)
            q = [vel[0, mine], vel[1, mine], sig[0, mine], sig[1, mine], sig[2, mine], strength[mine]]
            store(0, rows, q + [mask[mine].astype(jnp.float32), wind_f32[0, at], wind_f32[1, at], cot[0, mine], cot[1, mine]])
            q = []
            for field in range(NFLD):
                plane, to, width = slot_of(field)
                q.append(unstrip(land[0, plane, mine], land[1, plane, mine], to, width))
            store(1, rows, q)
        else:
            q = [ext[field, rows] for field in range(NFLD)]
            store(0, rows, [jnp.where(bottom, 0.0, x) for x in q] if r < PAD else q)

    def place_corners(end, turned):
        for group in range(3):
            q = [None] * NFLD
            for plane, slots in enumerate(corner_slots()):
                for of, field, to, width in slots:
                    if of == group:
                        q[field] = unstrip(corners[0, end, plane], corners[1, end, plane], to, width)
            q = [jnp.zeros(shape, jnp.float32) if x is None else x for x in q]
            if end == 1:
                q = [jnp.where(bottom, 0.0, x) for x in q]
            if turned:
                q = [-flip_tile(x) if field in ODD_FIELDS else flip_tile(x) for field, x in enumerate(q)]
            row = PAD + ROWS + GROUP * group if end == 0 else PAD - TILE - GROUP * group
            store(1, pl.ds(row, TILE), q)

    place_corners(1, False)
    pl.when(jnp.logical_not(top))(lambda: place_corners(0, False))
    pl.when(top)(lambda: place_corners(0, True))

    @pl.when(top)
    def _():
        for field in range(NFLD):
            old = [fld[field, 0, pl.ds(PAD + ROWS + t * TILE, TILE)] for t in range(3)]
            for t in range(3):
                new = flip_tile(old[2 - t])
                fld[field, 0, pl.ds(PAD + ROWS + t * TILE, TILE)] = -new if field in ODD_FIELDS else new

    for r in range(0, EXT, TILE):
        rows = pl.ds(r, TILE)
        row = band * ROWS + (r - PAD) + lax.broadcasted_iota(jnp.int32, shape, 0)
        total = ROWS * lat_count
        row = jnp.where(row >= total, 2 * total - 1 - row, row).astype(jnp.float32)
        half_f = 0.6 * ((2.0 * row + 1.0) / total - 1.0)
        scale = 1.5 / (2.25 + half_f * half_f)
        for plane in range(2):
            cover = fld[6, plane, rows]
            turn[0, plane, rows] = cover * (1.5 * scale)
            turn[1, plane, rows] = cover * (half_f * scale)

    def at(ref, lead, plane, r):
        if r < 0:
            return pltpu.roll(ref[lead + (plane, pl.ds(0, TILE))], 1, 0)
        if r > EXT - TILE:
            return pltpu.roll(ref[lead + (plane, pl.ds(EXT - TILE, TILE))], TILE - 1, 0)
        return ref[lead + (plane, pl.ds(r, TILE))]

    def lat_diff(ref, lead, r):
        return [at(ref, lead, p, r + 1) - at(ref, lead, p, r - 1) for p in range(2)]

    def lon_diff(ref, lead, r):
        here = [at(ref, lead, p, r) for p in range(2)]
        east = [pltpu.roll(x, COLS - 1, 1) for x in here]
        west = [pltpu.roll(x, 1, 1) for x in here]
        return [
            jnp.where(last_lane, east[1 - p], east[p]) - jnp.where(first_lane, west[1 - p], west[p])
            for p in range(2)
        ]

    start_value = start[0].astype(jnp.float32)
    for k in range(NSUB):
        src = fld if k == 0 else state
        left = NSUB - 1 - k
        keep = set(tiles_for(2 * k + 1))
        for r in tiles_for(11 + 2 * left):
            rows = pl.ds(r, TILE)
            dux = lon_diff(src, (0,), r)
            dvx = lon_diff(src, (1,), r)
            duy = lat_diff(src, (0,), r)
            dvy = lat_diff(src, (1,), r)
            for p in range(2):
                div = dux[p] + dvy[p]
                ten = dux[p] - dvy[p]
                she = duy[p] + dvx[p]
                inv = lax.rsqrt(div * div + 0.25 * (ten * ten + she * she) + 1.0)
                part = fld[5, p, rows]
                div = div * inv
                inv4 = 0.25 * inv
                ten = ten * inv4
                she = she * inv4
                if r in keep:
                    saved[k, 0, p, rows] = div
                    saved[k, 1, p, rows] = ten
                    saved[k, 2, p, rows] = she
                    saved[k, 3, p, rows] = part * inv
                cover = fld[6, p, rows]
                pull = div - 1.0
                state[2, p, rows] = cover * src[2, p, rows] + part * (pull + ten)
                state[3, p, rows] = cover * src[3, p, rows] + part * (pull - ten)
                state[4, p, rows] = cover * src[4, p, rows] + part * she
        weight = 0.5 * ((start_value + (k + 1)) / EVP_TOTAL)
        for r in tiles_for(0 if left == 0 else 10 + 2 * left):
            rows = pl.ds(r, TILE)
            dxx = lon_diff(state, (2,), r)
            dxy = lon_diff(state, (4,), r)
            dyx = lat_diff(state, (4,), r)
            dyy = lat_diff(state, (3,), r)
            for p in range(2):
                ru = src[0, p, rows] + (dxx[p] + dyx[p]) + weight * fld[7, p, rows]
                rv = src[1, p, rows] + (dxy[p] + dyy[p]) + weight * fld[8, p, rows]
                ca = turn[0, p, rows]
                cb = turn[1, p, rows]
                un = ca * ru + cb * rv
                vn = ca * rv - cb * ru
                if left == 0:
                    if p == 0:
                        final_vel[0, pl.ds(r - PAD, TILE)] = un
                        final_vel[1, pl.ds(r - PAD, TILE)] = vn
                else:
                    state[0, p, rows] = un
                    state[1, p, rows] = vn

    for r in tiles_for(BACK):
        rows = pl.ds(r, TILE)
        for p in range(2):
            gu = fld[9, p, rows]
            gv = fld[10, p, rows]
            ca = turn[0, p, rows]
            cb = turn[1, p, rows]
            back[0, p, rows] = ca * gu - cb * gv
            back[1, p, rows] = cb * gu + ca * gv

    for k in reversed(range(NSUB)):
        for r in tiles_for(2 * k + 1):
            rows = pl.ds(r, TILE)
            dux = lon_diff(back, (0,), r)
            dvx = lon_diff(back, (1,), r)
            duy = lat_diff(back, (0,), r)
            dvy = lat_diff(back, (1,), r)
            for p in range(2):
                gx = -dux[p]
                gy = -dvy[p]
                gz = -(duy[p] + dvx[p])
                if k < NSUB - 1:
                    gx = carry[0, p, rows] + gx
                    gy = carry[1, p, rows] + gy
                    gz = carry[2, p, rows] + gz
                both = gx + gy
                apart = gx - gy
                cover = fld[6, p, rows]
                if k > 0:
                    carry[0, p, rows] = cover * gx
                    carry[1, p, rows] = cover * gy
                    carry[2, p, rows] = cover * gz
                elif p == 0 and PAD <= r < PAD + ROWS:
                    out = pl.ds(r - PAD, TILE)
                    c8 = 0.125 * cover
                    sig_grad[0, out] = c8 * both
                    sig_grad[1, out] = c8 * apart
                    sig_grad[2, out] = (0.25 * cover) * gz
                div = saved[k, 0, p, rows]
                ten = saved[k, 1, p, rows]
                she = saved[k, 2, p, rows]
                part = saved[k, 3, p, rows]
                along = both * div + apart * ten + gz * she
                g_div = part * (both - along * div)
                g_ten = part * (0.25 * apart - along * ten)
                strain[0, p, rows] = g_div + g_ten
                strain[1, p, rows] = g_div - g_ten
                strain[2, p, rows] = part * (0.25 * gz - along * she)
        for r in tiles_for(2 * k):
            rows = pl.ds(r, TILE)
            dax = lon_diff(strain, (0,), r)
            dsx = lon_diff(strain, (2,), r)
            dsy = lat_diff(strain, (2,), r)
            dby = lat_diff(strain, (1,), r)
            for p in range(2):
                gu = back[0, p, rows] - (dax[p] + dsy[p])
                gv = back[1, p, rows] - (dsx[p] + dby[p])
                if k > 0:
                    ca = turn[0, p, rows]
                    cb = turn[1, p, rows]
                    back[0, p, rows] = ca * gu - cb * gv
                    back[1, p, rows] = cb * gu + ca * gv
                elif p == 0:
                    vel_grad[0, pl.ds(r - PAD, TILE)] = gu
                    vel_grad[1, pl.ds(r - PAD, TILE)] = gv


def evp_and_adjoint(lat_count, start, *operands):
    f32 = jnp.float32
    vmem = pl.BlockSpec(memory_space=pltpu.VMEM)
    return pl.pallas_call(
        partial(evp_kernel, lat_count),
        out_shape=(
            jax.ShapeDtypeStruct((2, ROWS, COLS), f32),
            jax.ShapeDtypeStruct((2, ROWS, COLS), f32),
            jax.ShapeDtypeStruct((3, ROWS, COLS), f32),
        ),
        in_specs=[pl.BlockSpec(memory_space=pltpu.SMEM)] + [vmem] * 9,
        out_specs=(vmem, vmem, vmem),
        scratch_shapes=[
            pltpu.VMEM((NFLD, 2, EXT, COLS), f32),
            pltpu.VMEM((5, 2, EXT, COLS), f32),
            pltpu.VMEM((2, 2, EXT, COLS), f32),
            pltpu.VMEM((NSUB, 4, 2, EXT, COLS), f32),
            pltpu.VMEM((2, 2, EXT, COLS), f32),
            pltpu.VMEM((3, 2, EXT, COLS), f32),
            pltpu.VMEM((3, 2, EXT, COLS), f32),
        ],
        compiler_params=pltpu.CompilerParams(vmem_limit_bytes=VMEM_LIMIT),
    )(start, *operands)


def shards(lon_count, lat_count, velocity, stress, strength, wind_stress, ice_mask, start_step, velocity_cotangent):
    block = (velocity, stress, strength, wind_stress, ice_mask, velocity_cotangent)
    halos = gather_halos(lon_count, lat_count, *(pltpu.with_memory_space_constraint(x, pltpu.HBM) for x in block))
    return evp_and_adjoint(lat_count, start_step, *block, *halos)


def solution(mesh):
    placed = (
        P(None, "lat", "lon"),
        P(None, "lat", "lon"),
        P("lat", "lon"),
        P(None, "lat", "lon"),
        P("lat", "lon"),
        P(),
        P(None, "lat", "lon"),
    )
    return jax.shard_map(
        partial(shards, mesh.shape["lon"], mesh.shape["lat"]),
        mesh=mesh,
        in_specs=placed,
        out_specs=(P(None, "lat", "lon"), P(None, "lat", "lon"), P(None, "lat", "lon")),
        check_vma=False,
    )
```
